256 devices in a mesh: ctx: 16 (over y_lo, z), head: 16 (over x, y_hi, core).
Axes of the slice: x: 4, y: 4 (y_hi: 2, y_lo: 2; y = y_hi * 2 + y_lo), z: 8, core: 2. Of those that a mesh axis runs over, the one named last changes fastest.
Arguments:
- q_noisy: bfloat16 [8192, 2048], P('ctx', 'head'), may hold values from -8 to 8
- k_noisy: bfloat16 [8192, 2048], P('ctx', 'head'), may hold values from -8 to 8
- v_noisy: bfloat16 [8192, 2048], P('ctx', 'head'), may hold values from -8 to 8
- k_clean: bfloat16 [8192, 2048], P('ctx', 'head'), may hold values from -8 to 8
- v_clean: bfloat16 [8192, 2048], P('ctx', 'head'), may hold values from -8 to 8
- out_weight: bfloat16 [2048, 4096], P('head'), may hold values from -0.1875 to 0.1875
- cotangent: bfloat16 [8192, 4096], P('ctx', 'head'), may hold values from -6 to 6
- noise_mask: int32 [8192], P('ctx'), may hold values from 0 to 1, as said below
- block_order: int32 [32], replicated, may hold values from 0 to 31, as said below
Outputs:
- mixed: bfloat16 [8192, 4096], P('ctx', 'head')
- grad_q_noisy: bfloat16 [8192, 2048], P('ctx', 'head')
- grad_k_noisy: bfloat16 [8192, 2048], P('ctx', 'head')
- grad_v_noisy: bfloat16 [8192, 2048], P('ctx', 'head')
- grad_k_clean: bfloat16 [8192, 2048], P('ctx', 'head')
- grad_v_clean: bfloat16 [8192, 2048], P('ctx', 'head')
- grad_out_weight: float32 [2048, 4096], P('head', 'ctx')
The draws below stay inside these ranges and needn't reach their ends.
Inputs may be any that keep to these rules, and one draw needn't show every extreme that they name: `noise_mask`: each block of 256 rows has its own share of ones. `block_order`: A permutation of the 32 block numbers; stored blocks 2j and 2j + 1 hold numbers that add up to 31.
All inputs are finite; a program needn't handle non-finite values.
Results may differ from the reference program's by a relative error of at most 0.04.
Values may be sent and summed in bfloat16 or wider, within the bound.
A program may use at most 128 MiB of HBM per device.

```python
import jax
import jax.numpy as jnp
from jax import lax

D = 4096
HEAD_DIM = 128
HEADS = 16
BLOCK = 256
TOK_DEV = 512
TOKENS = 8192
NBLOCKS = 32
N_HEAD = 16


def draw_q_noisy(key, part):
    key = jax.random.fold_in(key, 1)
    full_shape = (TOKENS, HEADS * HEAD_DIM)
    base = jnp.clip(1.4 * jax.random.normal(key, full_shape, jnp.float32), -8.0, 8.0)
    return base.astype(jnp.bfloat16)


def draw_k_noisy(key, part):
    key = jax.random.fold_in(key, 2)
    full_shape = (TOKENS, HEADS * HEAD_DIM)
    base = jnp.clip(1.4 * jax.random.normal(key, full_shape, jnp.float32), -8.0, 8.0)
    return base.astype(jnp.bfloat16)


def draw_k_clean(key, part):
    key = jax.random.fold_in(key, 3)
    full_shape = (TOKENS, HEADS * HEAD_DIM)
    base = jnp.clip(1.4 * jax.random.normal(key, full_shape, jnp.float32), -8.0, 8.0)
    return base.astype(jnp.bfloat16)


def draw_noise_mask(key, part):
    key = jax.random.fold_in(key, 7)
    rates = jax.random.randint(jax.random.fold_in(key, 1), (NBLOCKS,), 1, 65)
    coins = jax.random.randint(jax.random.fold_in(key, 2), (TOKENS,), 0, 64)
    return (coins < jnp.repeat(rates, BLOCK)).astype(jnp.int32)


def draw_block_order(key, part):
    key = jax.random.fold_in(key, 11)
    pair_count = NBLOCKS // 2
    chosen = jax.random.permutation(jax.random.fold_in(key, 1), jnp.arange(pair_count, dtype=jnp.int32))
    flips = jax.random.randint(jax.random.fold_in(key, 2), (pair_count,), 0, 2)
    first = jnp.where(flips == 1, chosen, NBLOCKS - 1 - chosen)
    second = NBLOCKS - 1 - first
    return jnp.stack([first, second], axis=1).reshape(NBLOCKS).astype(jnp.int32)


def spiked(drawn, own_key, source, target, shards_of, factor):
    owner, partner = [(jnp.arange(drawn.shape[position]) // (drawn.shape[position] // shards_of)).reshape([-1 if axis == position else 1 for axis in range(drawn.ndim)]) for position in (source, target)]
    chosen = jax.random.permutation(own_key, shards_of)[partner]
    strong = (owner == chosen) | (owner == (partner + shards_of // 2) % shards_of)
    return jnp.where(strong, factor * drawn, drawn)


def block_scale(own_key, shape, shards, smallest, largest):
    level = 1.0
    for dim, blocks in shards:
        steps = jax.random.uniform(jax.random.fold_in(jax.random.fold_in(own_key, 6), dim), (blocks,), jnp.float32, smallest / len(shards), largest / len(shards))
        level = level * jnp.repeat(jnp.exp(steps), shape[dim] // blocks).reshape((-1,) + (1,) * (len(shape) - 1 - dim))
    return level


def gaussian(stream_key, shape, width, bound, split=(), kind=jnp.bfloat16):
    entries = jax.random.normal(stream_key, shape, jnp.float32) * width
    if len(split) > 0:
        entries = block_scale(stream_key, shape, split, -0.22, 0.18) * entries
    return jnp.clip(entries, min=-bound, max=bound).astype(kind)


def gaussian_with(stream_key, shape, spread, reach, shards, heavy, held_as=jnp.bfloat16):
    entries = spread * jax.random.normal(stream_key, shape, jnp.float32)
    if shards:
        entries = entries * block_scale(stream_key, shape, shards, -0.22, 0.18)
    return jnp.clip(spiked(entries, jax.random.fold_in(stream_key, 3), *heavy), -reach, reach).astype(held_as)


def setup_inputs(seed: int = 0) -> dict:
    key_of = jax.random.split(jax.random.key(seed), 10)
    q_noisy = draw_q_noisy(jax.random.fold_in(key_of[9], 71), 0)
    k_noisy = draw_k_noisy(jax.random.fold_in(key_of[9], 71), 0)
    v_noisy = gaussian(key_of[2], (TOKENS, HEADS * HEAD_DIM), 2.0, 8.0, ((0, 16), (1, 16)))
    k_clean = draw_k_clean(jax.random.fold_in(key_of[9], 71), 0)
    v_clean = gaussian(key_of[4], (TOKENS, HEADS * HEAD_DIM), 2.0, 8.0, ((0, 16), (1, 16)))
    out_weight = gaussian_with(key_of[5], (HEADS * HEAD_DIM, D), (HEADS * HEAD_DIM) ** -0.5, 0.1875, ((0, 16),), (0, 1, 16, 2.0))
    cotangent = gaussian_with(key_of[6], (TOKENS, D), 1.0, 6.0, ((0, 16), (1, 16)), (0, 1, 16, 2.0))
    noise_mask = draw_noise_mask(jax.random.fold_in(key_of[9], 71), 0)
    block_order = draw_block_order(jax.random.fold_in(key_of[9], 71), 0)
    return {"q_noisy": q_noisy, "k_noisy": k_noisy, "v_noisy": v_noisy, "k_clean": k_clean, "v_clean": v_clean, "out_weight": out_weight, "cotangent": cotangent, "noise_mask": noise_mask, "block_order": block_order}


big_negative = -1.0e30


def head_slice(matrix, head):
    return lax.dynamic_slice_in_dim(matrix, head * HEAD_DIM, HEAD_DIM, 1)


def masked_scores(query_rows, key_rows, visible, score_scale):
    raw_scores = jnp.dot(query_rows, key_rows.T, preferred_element_type=jnp.float32) * score_scale
    return jnp.where(visible, raw_scores, big_negative)


def heads_to_rows(stacked):
    return jnp.transpose(stacked, (1, 2, 0, 3)).reshape(TOKENS, HEADS * HEAD_DIM)


def reference(q_noisy, k_noisy, v_noisy, k_clean, v_clean, out_weight, cotangent, noise_mask, block_order):
    score_scale = HEAD_DIM ** -0.5
    block_ids = jnp.repeat(block_order, BLOCK).astype(jnp.int32)
    group_count = TOKENS // TOK_DEV
    group_index = jnp.arange(group_count, dtype=jnp.int32)

    def forward_head(head):
        query_all = head_slice(q_noisy, head)
        near_all = head_slice(k_noisy, head)
        near_vals = head_slice(v_noisy, head)
        clean_keys = head_slice(k_clean, head)
        clean_vals = head_slice(v_clean, head)

        def forward_group(group):
            first_row = (group * TOK_DEV).astype(jnp.int32)
            query_rows = lax.dynamic_slice_in_dim(query_all, first_row, TOK_DEV, 0)
            near_keys = lax.dynamic_slice_in_dim(near_all, first_row, TOK_DEV, 0)
            near_values = lax.dynamic_slice_in_dim(near_vals, first_row, TOK_DEV, 0)
            query_ids = lax.dynamic_slice_in_dim(block_ids, first_row, TOK_DEV, 0)
            clean_scores = masked_scores(query_rows, clean_keys, block_ids[None, :] < query_ids[:, None], score_scale)
            near_scores = masked_scores(query_rows, near_keys, query_ids[None, :] == query_ids[:, None], score_scale)
            row_max = jnp.maximum(jnp.max(clean_scores, axis=1), jnp.max(near_scores, axis=1))
            clean_weights = jnp.exp(clean_scores - row_max[:, None])
            near_weights = jnp.exp(near_scores - row_max[:, None])
            row_sum = jnp.sum(clean_weights, axis=1) + jnp.sum(near_weights, axis=1)
            weighted = jnp.dot(clean_weights.astype(jnp.bfloat16), clean_vals, preferred_element_type=jnp.float32)
            weighted = weighted + jnp.dot(near_weights.astype(jnp.bfloat16), near_values, preferred_element_type=jnp.float32)
            attended_rows = (weighted / row_sum[:, None]).astype(jnp.bfloat16)
            return attended_rows, row_max + jnp.log(row_sum)

        return lax.map(forward_group, group_index)

    attended_heads, log_heads = lax.map(forward_head, jnp.arange(HEADS, dtype=jnp.int32))
    attended = heads_to_rows(attended_heads)
    log_rows = log_heads.reshape(HEADS, TOKENS)

    group_width = HEADS // N_HEAD * HEAD_DIM

    def add_group(summed, group):
        columns = lax.dynamic_slice_in_dim(attended, group * group_width, group_width, 1)
        weight_rows = lax.dynamic_slice_in_dim(out_weight, group * group_width, group_width, 0)
        partial_out = jnp.dot(columns, weight_rows, preferred_element_type=jnp.float32).astype(jnp.bfloat16)
        return summed + partial_out.astype(jnp.float32), None

    summed, unused = lax.scan(add_group, jnp.zeros((TOKENS, D), jnp.float32), jnp.arange(N_HEAD, dtype=jnp.int32))
    mixed = summed.astype(jnp.bfloat16)

    masked_cot = cotangent * noise_mask.astype(jnp.bfloat16)[:, None]
    grad_attended = jnp.dot(masked_cot, out_weight.T, preferred_element_type=jnp.float32).astype(jnp.bfloat16)
    grad_out_weight = jnp.dot(attended.T, masked_cot, preferred_element_type=jnp.float32)

    def backward_head(inputs):
        head, log_row = inputs
        query_all = head_slice(q_noisy, head)
        near_all = head_slice(k_noisy, head)
        near_vals = head_slice(v_noisy, head)
        clean_keys = head_slice(k_clean, head)
        clean_vals = head_slice(v_clean, head)
        grad_all = head_slice(grad_attended, head)
        attn_all = head_slice(attended, head)
        dot_all = jnp.sum(grad_all.astype(jnp.float32) * attn_all.astype(jnp.float32), axis=1)

        def backward_group(state_tuple, group):
            key_acc, value_acc = state_tuple
            first_row = (group * TOK_DEV).astype(jnp.int32)
            query_rows = lax.dynamic_slice_in_dim(query_all, first_row, TOK_DEV, 0)
            near_keys = lax.dynamic_slice_in_dim(near_all, first_row, TOK_DEV, 0)
            near_values = lax.dynamic_slice_in_dim(near_vals, first_row, TOK_DEV, 0)
            grad_rows = lax.dynamic_slice_in_dim(grad_all, first_row, TOK_DEV, 0)
            row_dot = lax.dynamic_slice_in_dim(dot_all, first_row, TOK_DEV, 0)
            log_total = lax.dynamic_slice_in_dim(log_row, first_row, TOK_DEV, 0)
            query_ids = lax.dynamic_slice_in_dim(block_ids, first_row, TOK_DEV, 0)
            clean_scores = masked_scores(query_rows, clean_keys, block_ids[None, :] < query_ids[:, None], score_scale)
            near_scores = masked_scores(query_rows, near_keys, query_ids[None, :] == query_ids[:, None], score_scale)
            clean_probs = jnp.exp(clean_scores - log_total[:, None])
            near_probs = jnp.exp(near_scores - log_total[:, None])
            clean_dp = jnp.dot(grad_rows, clean_vals.T, preferred_element_type=jnp.float32)
            near_dp = jnp.dot(grad_rows, near_values.T, preferred_element_type=jnp.float32)
            clean_grad = (clean_probs * (clean_dp - row_dot[:, None])).astype(jnp.bfloat16)
            near_grad = (near_probs * (near_dp - row_dot[:, None])).astype(jnp.bfloat16)
            query_grad = jnp.dot(clean_grad, clean_keys, preferred_element_type=jnp.float32)
            query_grad = (score_scale * (query_grad + jnp.dot(near_grad, near_keys, preferred_element_type=jnp.float32))).astype(jnp.bfloat16)
            near_key_grad = (score_scale * jnp.dot(near_grad.T, query_rows, preferred_element_type=jnp.float32)).astype(jnp.bfloat16)
            near_value_grad = jnp.dot(near_probs.astype(jnp.bfloat16).T, grad_rows, preferred_element_type=jnp.float32).astype(jnp.bfloat16)
            key_part = (score_scale * jnp.dot(clean_grad.T, query_rows, preferred_element_type=jnp.float32)).astype(jnp.bfloat16)
            value_part = jnp.dot(clean_probs.astype(jnp.bfloat16).T, grad_rows, preferred_element_type=jnp.float32).astype(jnp.bfloat16)
            new_state = (key_acc + key_part.astype(jnp.float32), value_acc + value_part.astype(jnp.float32))
            return new_state, (query_grad, near_key_grad, near_value_grad)

        zero_rows = jnp.zeros((TOKENS, HEAD_DIM), jnp.float32)
        final_state, per_group = lax.scan(backward_group, (zero_rows, zero_rows), group_index)
        return final_state[0].astype(jnp.bfloat16), final_state[1].astype(jnp.bfloat16), per_group[0], per_group[1], per_group[2]

    key_heads, value_heads, query_heads, near_key_heads, near_value_heads = lax.map(
        backward_head, (jnp.arange(HEADS, dtype=jnp.int32), log_rows))
    grad_k_clean = jnp.transpose(key_heads, (1, 0, 2)).reshape(TOKENS, HEADS * HEAD_DIM)
    grad_v_clean = jnp.transpose(value_heads, (1, 0, 2)).reshape(TOKENS, HEADS * HEAD_DIM)
    return (mixed, heads_to_rows(query_heads), heads_to_rows(near_key_heads), heads_to_rows(near_value_heads),
            grad_k_clean, grad_v_clean, grad_out_weight)
```

```python
import functools

import jax
import jax.numpy as jnp
from jax import lax
from jax.experimental import pallas as pl
from jax.experimental.pallas import tpu as pltpu
from jax.sharding import PartitionSpec as P

BLOCK = 256
HEAD_DIM = 128
SCALE = HEAD_DIM**-0.5
SCALE2 = SCALE * 1.4426950408889634
EMPTY = -1e30
NZ = 8
MESH = pl.DeviceIdType.MESH
BF = jnp.bfloat16
F32 = jnp.float32


def nt(a, b):
    return lax.dot_general(a, b, (((1,), (1,)), ((), ())), preferred_element_type=F32)


def nn(a, b):
    return lax.dot_general(a, b, (((1,), (0,)), ((), ())), preferred_element_type=F32)


def remote(src, dst, send_sem, recv_sem, device):
    return pltpu.make_async_remote_copy(
        src_ref=src,
        dst_ref=dst,
        send_sem=send_sem,
        recv_sem=recv_sem,
        device_id=device,
        device_id_type=MESH,
    )


def forward_tile(keys, values_t, queries, state):
    row_max, row_sum, acc = state
    scores = nt(keys, queries)
    new_max = jnp.maximum(row_max, jnp.max(scores, axis=0, keepdims=True))
    weights = jnp.exp2((scores - new_max) * SCALE2)
    shrink = jnp.exp2((row_max - new_max) * SCALE2)
    new_sum = row_sum * shrink + jnp.sum(weights, axis=0, keepdims=True)
    new_acc = acc * shrink + nn(values_t, weights.astype(BF))
    return new_max, new_sum, new_acc


def backward_tile(keys, values, keys_t, queries, grads, log_total, row_dot):
    probs = jnp.exp2(nt(keys, queries) * SCALE2 - log_total)
    grad_probs = nt(values, grads)
    grad_scores = (probs * (grad_probs - row_dot)).astype(BF)
    return nn(grad_scores, queries), nn(probs.astype(BF), grads), nn(keys_t, grad_scores)


def kernel(
    order, mask, q, kn, vn, kc, vc, w, cot,
    mixed, gq, gkn, gvn, gkc, gvc, gw,
    qs, kns, vns, kv, kt, vt, knt, vnt, ml, ml_in, acc, acc_out, acc_in,
    cotm, cot_all, w_cols, att_t, att_all, do_acc, dos, ld, dq, dq_out, dq_in,
    cb, rs_out, rs_in, gy_out, gy_in, g_out, g_in, stage,
    kv_ss, kv_rs, y_ss, y_rs, gy_ss, gy_rs, c_ss, c_rs, a_ss, a_rs, w_ss, w_rs,
    r_ss, r_rs, g_ss, g_rs,
):
    c = lax.axis_index("ctx")
    h = lax.axis_index("head")
    yl, z = c // NZ, c % NZ
    x, yh, co = h // 4, (h // 2) % 2, h % 2
    sends = []

    def go(copy):
        copy.start()
        sends.append(copy)

    def head_of(x_, yh_, co_):
        return x_ * 4 + yh_ * 2 + co_

    z_dev = [(yl * NZ + (z + 1) % NZ, h), (yl * NZ + (z + NZ - 1) % NZ, h)]
    y_ctx = (1 - yl) * NZ + z
    y_dev = (y_ctx, h)
    heads = [(h + k) % 16 for k in range(1, 16)]

    barrier = pltpu.get_barrier_semaphore()
    for dev in z_dev + [y_dev] + [(c, p) for p in heads]:
        pl.semaphore_signal(barrier, inc=1, device_id=dev, device_id_type=MESH)

    swap = order[2 * c] > order[2 * c + 1]

    def in_order(ref, i):
        first, second = ref[:BLOCK, :], ref[BLOCK:, :]
        return jnp.where(swap, first, second) if i else jnp.where(swap, second, first)

    def low_id(ctx):
        return jnp.minimum(order[2 * ctx], order[2 * ctx + 1])

    for i in range(2):
        kv[z, 0, i] = in_order(kc, i)
        kv[z, 1, i] = in_order(vc, i)
        qs[0, i] = in_order(q, i)
    row_id = lax.broadcasted_iota(jnp.int32, (128, 128), 0)
    col_id = lax.broadcasted_iota(jnp.int32, (128, 128), 1)
    for b in range(4):
        flags = jnp.broadcast_to(mask[b : b + 1, :].astype(F32), (128, 128))
        column = jnp.sum(jnp.where(row_id == col_id, flags, 0.0), axis=1, keepdims=True)
        rows = slice(b * 128, (b + 1) * 128)
        cotm[rows, :] = (cot[rows, :].astype(F32) * column).astype(BF)
    for i in range(2):
        cot_all[h, i * BLOCK : (i + 1) * BLOCK, :] = in_order(cotm, i)

    pl.semaphore_wait(barrier, 18)

    def kv_copy(d, s, t):
        slot = (z + NZ - (s - 1)) % NZ if d == 0 else (z + s - 1) % NZ
        return remote(
            kv.at[slot, t], kv.at[slot, t], kv_ss.at[d, s - 1, t], kv_rs.at[d, s - 1, t], z_dev[d]
        )

    def kv_wait(d, s, t):
        slot = (z + NZ - s) % NZ if d == 0 else (z + s) % NZ
        remote(
            kv.at[slot, t], kv.at[slot, t], kv_ss.at[d, s - 1, t], kv_rs.at[d, s - 1, t], z_dev[d]
        ).wait_recv()

    def head_copy(buf, ss, rs, index, slot, dev_head):
        return remote(buf.at[slot], buf.at[slot], ss.at[index], rs.at[index], (c, dev_head))

    yh_head = head_of(x, 1 - yh, co)
    sib = head_of(x, yh, 1 - co)

    def x_head(k, yh_, co_):
        return head_of((x + k) % 4, yh_, co_)

    def gather_begin(buf, ss, rs):
        go(head_copy(buf, ss, rs, 0, h, yh_head))
        for k in (1, 3, 2):
            go(head_copy(buf, ss, rs, k, h, x_head(k, yh, co)))
        go(head_copy(buf, ss, rs, 7, h, sib))

    def gather_second(buf, ss, rs):
        head_copy(buf, ss, rs, 0, yh_head, yh_head).wait_recv()
        for k in (1, 3, 2):
            go(head_copy(buf, ss, rs, 3 + k, yh_head, x_head(k, yh, co)))
        go(head_copy(buf, ss, rs, 8, yh_head, sib))

    def gather_pass(buf, ss, rs, second):
        for k in (1, 3, 2):
            index = 3 * second + k
            slot = head_of((x + 4 - k) % 4, 1 - yh if second else yh, co)
            head_copy(buf, ss, rs, index, slot, yh_head).wait_recv()
            go(head_copy(buf, ss, rs, 8 + index, slot, sib))

    def gather_end(buf, ss, rs):
        slots = [sib, head_of(x, 1 - yh, 1 - co)]
        slots += [head_of((x + 4 - k) % 4, yh, 1 - co) for k in (1, 2, 3)]
        slots += [head_of((x + 4 - k) % 4, 1 - yh, 1 - co) for k in (1, 2, 3)]
        for j, slot in enumerate(slots):
            head_copy(buf, ss, rs, 7 + j, slot, sib).wait_recv()

    def y_copy(index, src, dst):
        return remote(src, dst, y_ss.at[index], y_rs.at[index], y_dev)

    for t in range(2):
        for d in range(2):
            go(kv_copy(d, 1, t))
    q_copy = y_copy(0, qs.at[0], qs.at[1])
    go(q_copy)
    gather_begin(cot_all, c_ss, c_rs)

    for i in range(2):
        kns[i] = in_order(kn, i)
        vns[i] = in_order(vn, i)
        knt[i] = kns[i].T
        vnt[i] = vns[i].T

    def transpose_slot(slot):
        for i in range(2):
            kt[slot, i] = kv[slot, 0, i].T
            vt[slot, i] = kv[slot, 1, i].T

    def get_state(qd, i):
        return ml[qd, i], ml[qd, 2 + i], acc[qd, i]

    def put_state(qd, i, state):
        ml[qd, i], ml[qd, 2 + i] = (jnp.broadcast_to(v, (8, BLOCK)) for v in state[:2])
        acc[qd, i] = state[2]

    def rows_of(state):
        return state[0][:1], state[1][:1], state[2]

    def seen_high(qd, slot):
        q_ctx = (yl + qd * (1 - 2 * yl)) * NZ + z
        return low_id(yl * NZ + slot) > low_id(q_ctx)

    def forward_pair(qd, slot):
        high = seen_high(qd, slot)
        q_low, q_high = qs[qd, 0], qs[qd, 1]
        state_high = forward_tile(
            kv[slot, 0, 0], vt[slot, 0], q_high, rows_of(get_state(qd, 1))
        )
        state_low = rows_of(get_state(qd, 0))
        state = tuple(jnp.where(high, a, b) for a, b in zip(state_high, state_low))
        state = forward_tile(
            jnp.where(high, kv[slot, 0, 1], kv[slot, 0, 0]),
            jnp.where(high, vt[slot, 1], vt[slot, 0]),
            jnp.where(high, q_high, q_low),
            state,
        )
        put_state(qd, 0, tuple(jnp.where(high, b, a) for a, b in zip(state, state_low)))
        put_state(qd, 1, tuple(jnp.where(high, a, b) for a, b in zip(state, state_high)))

    empty = (
        jnp.full((1, BLOCK), EMPTY, F32),
        jnp.zeros((1, BLOCK), F32),
        jnp.zeros((HEAD_DIM, BLOCK), F32),
    )
    transpose_slot(z)
    for i in range(2):
        state = forward_tile(kns[i], vnt[i], qs[0, i], empty)
        if i == 1:
            state = forward_tile(kv[z, 0, 0], vt[z, 0], qs[0, 1], state)
        put_state(0, i, state)
        put_state(1, i, empty)
    q_copy.wait_recv()
    forward_pair(1, z)

    for s in range(1, 5):
        for t in range(2):
            for d in range(2):
                if s < 4 or t == d:
                    kv_wait(d, s, t)
                    if s < 3 or (s == 3 and t == d):
                        go(kv_copy(d, s + 1, t))
        if s < 4:

            def step(i, carry, s=s):
                slot = (z + NZ + (2 * i - 1) * s) % NZ
                transpose_slot(slot)
                forward_pair(0, slot)
                forward_pair(1, slot)
                return carry

            lax.fori_loop(0, 2, step, 0)
        else:
            slot = (z + 4) % NZ
            transpose_slot(slot)
            forward_pair(1, slot)
            for i in range(2):
                acc_out[i] = acc[1, i].astype(BF)
            ml_copy = y_copy(1, ml.at[1], ml_in)
            acc_copy = y_copy(2, acc_out, acc_in)
            go(ml_copy)
            go(acc_copy)
            forward_pair(0, slot)
        if s == 2:
            gather_second(cot_all, c_ss, c_rs)
        if s == 3:
            gather_pass(cot_all, c_ss, c_rs, 0)
    gather_pass(cot_all, c_ss, c_rs, 1)

    for k in range(1, 16):
        go(
            remote(
                w.at[:, pl.ds(pl.multiple_of(heads[k - 1] * 256, 256), 256)],
                w_cols.at[h],
                w_ss.at[k - 1],
                w_rs.at[k - 1],
                (c, heads[k - 1]),
            )
        )
    w_cols[h] = w[:, pl.ds(pl.multiple_of(h * 256, 256), 256)]

    gather_end(cot_all, c_ss, c_rs)
    do_acc[...] = jnp.zeros_like(do_acc)

    def add_piece(p, carry):
        columns = pl.ds(pl.multiple_of(p * 256, 256), 256)
        do_acc[...] += nt(cot_all[p], w[:, columns])
        return carry

    lax.fori_loop(0, 16, add_piece, 0)
    for i in range(2):
        dos[0, i] = do_acc[i * BLOCK : (i + 1) * BLOCK, :].astype(BF)
    do_copy = y_copy(3, dos.at[0], dos.at[1])
    go(do_copy)

    ml_copy.wait_recv()
    acc_copy.wait_recv()
    for i in range(2):
        own_max, own_sum, own_acc = rows_of(get_state(0, i))
        other_max, other_sum = ml_in[i][:1], ml_in[2 + i][:1]
        top = jnp.maximum(own_max, other_max)
        own_part = jnp.exp2((own_max - top) * SCALE2)
        other_part = jnp.exp2((other_max - top) * SCALE2)
        total = own_sum * own_part + other_sum * other_part
        weighted = own_acc * own_part + acc_in[i].astype(F32) * other_part
        attended_t = (weighted / total).astype(BF)
        att_t[:, i * BLOCK : (i + 1) * BLOCK] = attended_t
        att_all[h, i * BLOCK : (i + 1) * BLOCK, :] = attended_t.T
        grads_t = dos[0, i].T.astype(F32)
        row_dot = jnp.sum(grads_t * attended_t.astype(F32), axis=0, keepdims=True)
        ld[0, i] = jnp.broadcast_to(top * SCALE2 + jnp.log2(total), (8, BLOCK))
        ld[0, 2 + i] = jnp.broadcast_to(row_dot, (8, BLOCK))
    ld_copy = y_copy(4, ld.at[0], ld.at[1])
    go(ld_copy)
    gather_begin(att_all, a_ss, a_rs)

    def gy_slot(j):
        return (z + (4, 3, 5, 2, 6, 1, 7, 0)[j]) % NZ

    gy_copies = []
    for j in range(8):
        slot = gy_slot(j)
        gy_out[j] = nn(att_t[...], cot_all[(1 - yl) * NZ + slot]).astype(BF)
        gy_copies.append(remote(gy_out.at[j], gy_in.at[j], gy_ss.at[j], gy_rs.at[j], y_dev))
        go(gy_copies[-1])

    for i in range(2):
        key_term, value_term, query_term = backward_tile(
            kns[i], vns[i], knt[i], qs[0, i], dos[0, i], ld[0, i][:1], ld[0, 2 + i][:1]
        )
        stage[0, i] = (key_term * SCALE).astype(BF)
        stage[1, i] = value_term.astype(BF)
        dq[0, i] = query_term
        dq[1, i] = jnp.zeros_like(query_term)

    def unsort(index, out):
        for b in range(2):
            rows = jnp.where(swap, stage[index, 1 - b], stage[index, b])
            out[b * BLOCK : (b + 1) * BLOCK, :] = rows

    unsort(0, gkn)
    unsort(1, gvn)

    do_copy.wait_recv()
    ld_copy.wait_recv()

    def backward_pair(d, qd, slot, same):
        low, high = (
            backward_tile(
                kv[slot, 0, 0], kv[slot, 1, 0], kt[slot, 0],
                qs[qd, 1], dos[qd, 1], ld[qd, 1][:1], ld[qd, 3][:1],
            ),
            None,
        )
        if same:
            cb[d, 0, 0] = low[0]
            cb[d, 1, 0] = low[1]
            cb[d, 0, 1] = jnp.zeros_like(low[0])
            cb[d, 1, 1] = jnp.zeros_like(low[1])
            dq[qd, 1] += low[2]
            return
        pick = seen_high(qd, slot)

        def chosen(first, second):
            return jnp.where(pick, second, first)

        high = backward_tile(
            chosen(kv[slot, 0, 0], kv[slot, 0, 1]),
            chosen(kv[slot, 1, 0], kv[slot, 1, 1]),
            chosen(kt[slot, 0], kt[slot, 1]),
            chosen(qs[qd, 0], qs[qd, 1]),
            chosen(dos[qd, 0], dos[qd, 1]),
            chosen(ld[qd, 0][:1], ld[qd, 1][:1]),
            chosen(ld[qd, 2][:1], ld[qd, 3][:1]),
        )
        to_high = pick.astype(F32)
        to_low = 1.0 - to_high
        for t in range(2):
            new_low = low[t] + high[t] * to_low
            new_high = high[t] * to_high
            if qd == 0:
                cb[d, t, 0] = new_low
                cb[d, t, 1] = new_high
            else:
                cb[d, t, 0] += new_low
                cb[d, t, 1] += new_high
        dq[qd, 0] += high[2] * to_low
        dq[qd, 1] += low[2] + high[2] * to_high

    def contributions(s):
        if s in (0, 4):
            slot = (z + 4 - s) % NZ
            backward_pair(0, 0, slot, s == 4)
            backward_pair(0, 1, slot, False)
        else:

            def step(d, carry):
                slot = (z + NZ + (1 - 2 * d) * (4 - s)) % NZ
                backward_pair(d, 0, slot, False)
                backward_pair(d, 1, slot, False)
                return carry

            lax.fori_loop(0, 2, step, 0)

    factors = (SCALE, 1.0)

    def rs_copy(d, s, t):
        return remote(
            rs_out.at[d, s, t], rs_in.at[d, s, t], r_ss.at[d, s, t], r_rs.at[d, s, t], z_dev[d]
        )

    def g_copy(d, s):
        rows = pl.ds(64 * d, 64) if s == 0 else pl.ds(0, 128)
        return remote(
            g_out.at[d, s, rows], g_in.at[d, s, rows], g_ss.at[d, s], g_rs.at[d, s], z_dev[d]
        )

    def g_piece(j):
        gy_copies[j].wait_recv()
        own = nn(att_t[...], cot_all[yl * NZ + gy_slot(j)])
        return own + gy_in[j].astype(F32)

    contributions(0)
    for t in range(2):
        for i in range(2):
            rs_out[t, 0, t, i] = (cb[0, t, i] * factors[t]).astype(BF)
        go(rs_copy(t, 0, t))

    for s in range(1, 5):
        contributions(s)
        if s == 1:
            piece = g_piece(0).astype(BF)
            for d in range(2):
                g_out[d, 0] = piece
                go(g_copy(d, 0))
        else:
            for d in range(2):
                g_copy(d, s - 2).wait_recv()
                piece = g_piece(2 * (s - 1) - 1 + d)
                if s == 2:
                    half = slice(64 * d, 64 * d + 64)
                    rest = slice(64 - 64 * d, 128 - 64 * d)
                    g_out[d, 1, half] = (piece[half] + g_in[d, 0, half].astype(F32)).astype(BF)
                    g_out[d, 1, rest] = piece[rest].astype(BF)
                else:
                    g_out[d, s - 1] = (piece + g_in[d, s - 2].astype(F32)).astype(BF)
                go(g_copy(d, s - 1))
        if s < 4:
            for t in range(2):
                for d in range(2):
                    if s == 1 and t != d:
                        for i in range(2):
                            rs_out[d, 1, t, i] = (cb[d, t, i] * factors[t]).astype(BF)
                    else:
                        rs_copy(d, s - 1, t).wait_recv()
                        for i in range(2):
                            rs_out[d, s, t, i] = (
                                cb[d, t, i] * factors[t] + rs_in[d, s - 1, t, i].astype(F32)
                            ).astype(BF)
                    go(rs_copy(d, s, t))
        if s == 1:
            gather_second(att_all, a_ss, a_rs)
        if s == 2:
            gather_pass(att_all, a_ss, a_rs, 0)
        if s == 3:
            gather_pass(att_all, a_ss, a_rs, 1)

    for i in range(2):
        dq_out[i] = (dq[1, i] * SCALE).astype(BF)
    dq_copy = y_copy(5, dq_out, dq_in)
    go(dq_copy)

    gather_end(att_all, a_ss, a_rs)
    for k in range(1, 16):
        source = (h + 16 - k) % 16
        remote(
            w.at[:, pl.ds(0, 256)], w_cols.at[source], w_ss.at[k - 1], w_rs.at[k - 1], (c, source)
        ).wait_recv()
    total = nn(att_all[0], w_cols[0])
    for p in range(1, 16):
        total = total + nn(att_all[p], w_cols[p])
    cotm[...] = total.astype(BF)
    for b in range(2):
        mixed[b * BLOCK : (b + 1) * BLOCK, :] = in_order(cotm, b)

    dq_copy.wait_recv()
    for i in range(2):
        stage[2, i] = (dq[0, i] * SCALE + dq_in[i].astype(F32)).T.astype(BF)
    unsort(2, gq)

    piece = g_piece(7)
    for d in range(2):
        g_copy(d, 3).wait_recv()
        piece = piece + g_in[d, 3].astype(F32)
    gw[...] = piece

    for t in range(2):
        for d in range(2):
            rs_copy(d, 3, t).wait_recv()
        for i in range(2):
            stage[3 + t, i] = (
                cb[0, t, i] * factors[t]
                + rs_in[0, 3, t, i].astype(F32)
                + rs_in[1, 3, t, i].astype(F32)
            ).astype(BF)
    unsort(3, gkc)
    unsort(4, gvc)

    for copy in sends:
        copy.wait_send()


def per_device(q, kn, vn, kc, vc, w, cot, noise_mask, block_order):
    vmem = pl.BlockSpec(memory_space=pltpu.VMEM)
    smem = pl.BlockSpec(memory_space=pltpu.SMEM)
    rows, width = q.shape
    blk = (BLOCK, HEAD_DIM)
    tblk = (HEAD_DIM, BLOCK)
    dma = pltpu.SemaphoreType.DMA
    narrow = jax.ShapeDtypeStruct((rows, width), BF)
    scratch = [
        pltpu.VMEM((2, 2) + blk, BF),
        pltpu.VMEM((2,) + blk, BF),
        pltpu.VMEM((2,) + blk, BF),
        pltpu.VMEM((NZ, 2, 2) + blk, BF),
        pltpu.VMEM((NZ, 2) + tblk, BF),
        pltpu.VMEM((NZ, 2) + tblk, BF),
        pltpu.VMEM((2,) + tblk, BF),
        pltpu.VMEM((2,) + tblk, BF),
        pltpu.VMEM((2, 4, 8, BLOCK), F32),
        pltpu.VMEM((4, 8, BLOCK), F32),
        pltpu.VMEM((2, 2) + tblk, F32),
        pltpu.VMEM((2,) + tblk, BF),
        pltpu.VMEM((2,) + tblk, BF),
        pltpu.VMEM((rows, 256), BF),
        pltpu.VMEM((16, rows, 256), BF),
        pltpu.VMEM((16, HEAD_DIM, 256), BF),
        pltpu.VMEM((HEAD_DIM, rows), BF),
        pltpu.VMEM((16, rows, HEAD_DIM), BF),
        pltpu.VMEM((rows, HEAD_DIM), F32),
        pltpu.VMEM((2, 2) + blk, BF),
        pltpu.VMEM((2, 4, 8, BLOCK), F32),
        pltpu.VMEM((2, 2) + tblk, F32),
        pltpu.VMEM((2,) + tblk, BF),
        pltpu.VMEM((2,) + tblk, BF),
        pltpu.VMEM((2, 2, 2) + blk, F32),
        pltpu.VMEM((2, 4, 2, 2) + blk, BF),
        pltpu.VMEM((2, 4, 2, 2) + blk, BF),
        pltpu.VMEM((8, HEAD_DIM, 256), BF),
        pltpu.VMEM((8, HEAD_DIM, 256), BF),
        pltpu.VMEM((2, 4, HEAD_DIM, 256), BF),
        pltpu.VMEM((2, 4, HEAD_DIM, 256), BF),
        pltpu.VMEM((5, 2) + blk, BF),
        dma((2, 4, 2)), dma((2, 4, 2)),
        dma((6,)), dma((6,)),
        dma((8,)), dma((8,)),
        dma((15,)), dma((15,)),
        dma((15,)), dma((15,)),
        dma((15,)), dma((15,)),
        dma((2, 4, 2)), dma((2, 4, 2)),
        dma((2, 4)), dma((2, 4)),
    ]
    return pl.pallas_call(
        kernel,
        out_shape=(
            jax.ShapeDtypeStruct(cot.shape, BF),
            narrow, narrow, narrow, narrow, narrow,
            jax.ShapeDtypeStruct((HEAD_DIM, 256), F32),
        ),
        in_specs=[smem] + [vmem] * 8,
        out_specs=(vmem,) * 7,
        scratch_shapes=scratch,
        compiler_params=pltpu.CompilerParams(
            collective_id=0, has_side_effects=True, vmem_limit_bytes=56 * 2**20
        ),
        name="block_attention",
    )(block_order, noise_mask.reshape(4, 128), q, kn, vn, kc, vc, w, cot)


def solution(mesh):
    spread = P("ctx", "head")
    return jax.shard_map(
        per_device,
        mesh=mesh,
        in_specs=(spread,) * 5 + (P("head", None), spread, P("ctx"), P()),
        out_specs=(spread,) * 6 + (P("head", "ctx"),),
        check_vma=False,
    )
```

```python
import functools

import jax
import jax.numpy as jnp
from jax import lax
from jax.experimental import pallas as pl
from jax.experimental.pallas import tpu as pltpu
from jax.sharding import PartitionSpec as P

BLOCK = 256
HEAD_DIM = 128
SCALE = HEAD_DIM**-0.5
SCALE2 = SCALE * 1.4426950408889634
EMPTY = -1e30
NZ = 8
MESH = pl.DeviceIdType.MESH
BF = jnp.bfloat16
F32 = jnp.float32


def nt(a, b):
    return lax.dot_general(a, b, (((1,), (1,)), ((), ())), preferred_element_type=F32)


def nn(a, b):
    return lax.dot_general(a, b, (((1,), (0,)), ((), ())), preferred_element_type=F32)


def remote(src, dst, send_sem, recv_sem, device):
    return pltpu.make_async_remote_copy(
        src_ref=src,
        dst_ref=dst,
        send_sem=send_sem,
        recv_sem=recv_sem,
        device_id=device,
        device_id_type=MESH,
    )


def forward_tile(keys, values_t, queries, state):
    row_max, row_sum, acc = state
    scores = nt(keys, queries)
    new_max = jnp.maximum(row_max, jnp.max(scores, axis=0, keepdims=True))
    weights = jnp.exp2((scores - new_max) * SCALE2)
    shrink = jnp.exp2((row_max - new_max) * SCALE2)
    new_sum = row_sum * shrink + jnp.sum(weights, axis=0, keepdims=True)
    new_acc = acc * shrink + nn(values_t, weights.astype(BF))
    return new_max, new_sum, new_acc


def backward_tile(keys, values, keys_t, queries, grads, log_total, row_dot):
    probs = jnp.exp2(nt(keys, queries) * SCALE2 - log_total)
    grad_probs = nt(values, grads)
    grad_scores = (probs * (grad_probs - row_dot)).astype(BF)
    return nn(grad_scores, queries), nn(probs.astype(BF), grads), nn(keys_t, grad_scores)


def kernel(
    order, mask, q_in, kn_in, vn_in, kc_in, vc_in, w_in, cot_in,
    mixed, gq, gkn, gvn, gkc, gvc, gw,
    q, kn, vn, kc, vc, w, cot,
    qs, kns, vns, kv, kt, vt, knt, vnt, ml, ml_in, acc, acc_out, acc_in,
    cotm, cot_all, w_cols, w_mid, att_t, att_all, do_acc, dos, ld, dq, dq_out, dq_in,
    cb, rs_out, rs_in, gy_out, gy_in, g_out, g_in, stage, finals, mixed_final, gw_final,
    in_sem, out_sem,
    kv_ss, kv_rs, y_ss, y_rs, gy_ss, gy_rs, c_ss, c_rs, a_ss, a_rs, wm_ss, wm_rs, w_ss, w_rs,
    r_ss, r_rs, g_ss, g_rs,
):
    c = lax.axis_index("ctx")
    h = lax.axis_index("head")
    yl, z = c // NZ, c % NZ
    x, yh, co = h // 4, (h // 2) % 2, h % 2
    sends = []

    def go(copy):
        copy.start()
        sends.append(copy)

    def head_of(x_, yh_, co_):
        return x_ * 4 + yh_ * 2 + co_

    z_dev = [(yl * NZ + (z + 1) % NZ, h), (yl * NZ + (z + NZ - 1) % NZ, h)]
    y_ctx = (1 - yl) * NZ + z
    y_dev = (y_ctx, h)
    heads = [head_of((x + k) % 4, yh, co_) for k in range(1, 4) for co_ in range(2)]
    heads += [head_of(x, yh, 1 - co), head_of(x, 1 - yh, co)]

    loads = [
        pltpu.make_async_copy(src, dst, in_sem.at[i])
        for i, (src, dst) in enumerate(
            ((kc_in, kc), (vc_in, vc), (cot_in, cot), (q_in, q), (kn_in, kn), (vn_in, vn), (w_in, w))
        )
    ]
    for load in loads:
        load.start()
    stores = []

    def put(src, dst):
        store = pltpu.make_async_copy(src, dst, out_sem.at[len(stores)])
        store.start()
        stores.append(store)

    barrier = pltpu.get_barrier_semaphore()
    for dev in z_dev + [y_dev] + [(c, p) for p in heads]:
        pl.semaphore_signal(barrier, inc=1, device_id=dev, device_id_type=MESH)

    swap = order[2 * c] > order[2 * c + 1]

    def in_order(ref, i):
        first, second = ref[:BLOCK, :], ref[BLOCK:, :]
        return jnp.where(swap, first, second) if i else jnp.where(swap, second, first)

    def low_id(ctx):
        return jnp.minimum(order[2 * ctx], order[2 * ctx + 1])

    loads[0].wait()
    loads[1].wait()
    for i in range(2):
        kv[z, 0, i] = in_order(kc, i)
        kv[z, 1, i] = in_order(vc, i)
    loads[2].wait()
    row_id = lax.broadcasted_iota(jnp.int32, (128, 128), 0)
    col_id = lax.broadcasted_iota(jnp.int32, (128, 128), 1)
    for b in range(4):
        flags = jnp.broadcast_to(mask[b : b + 1, :].astype(F32), (128, 128))
        column = jnp.sum(jnp.where(row_id == col_id, flags, 0.0), axis=1, keepdims=True)
        rows = slice(b * 128, (b + 1) * 128)
        cotm[rows, :] = (cot[rows, :].astype(F32) * column).astype(BF)
    for i in range(2):
        cot_all[h, i * BLOCK : (i + 1) * BLOCK, :] = in_order(cotm, i)

    loads[3].wait()
    for i in range(2):
        qs[0, i] = in_order(q, i)

    pl.semaphore_wait(barrier, 11)

    def kv_chunk(d, s, t, i, slot):
        chunk = kv.at[slot, t, i]
        return remote(chunk, chunk, kv_ss.at[d, s - 1, t, i], kv_rs.at[d, s - 1, t, i], z_dev[d])

    def kv_copy(d, s, t, i):
        return kv_chunk(d, s, t, i, (z + NZ - (s - 1)) % NZ if d == 0 else (z + s - 1) % NZ)

    def kv_wait(d, s, t, i):
        kv_chunk(d, s, t, i, (z + NZ - s) % NZ if d == 0 else (z + s) % NZ).wait_recv()

    def head_copy(buf, ss, rs, index, slot, dev_head):
        return remote(buf.at[slot], buf.at[slot], ss.at[index], rs.at[index], (c, dev_head))

    yh_head = head_of(x, 1 - yh, co)
    sib = head_of(x, yh, 1 - co)

    def x_head(k, yh_, co_):
        return head_of((x + k) % 4, yh_, co_)

    def x_copy(buf, ss, rs, second, d, half, slot):
        rows = pl.ds(256 * d, 256) if half else pl.ds(0, 512)
        index = 1 + 4 * second + 2 * half + d
        chunk = buf.at[slot, rows]
        dev = (c, x_head(1 if d == 0 else 3, yh, co))
        return remote(chunk, chunk, ss.at[index], rs.at[index], dev)

    def gather_begin(buf, ss, rs):
        go(head_copy(buf, ss, rs, 0, h, yh_head))
        for d in range(2):
            go(x_copy(buf, ss, rs, 0, d, 0, h))
        go(head_copy(buf, ss, rs, 9, h, sib))

    def gather_second(buf, ss, rs):
        head_copy(buf, ss, rs, 0, yh_head, yh_head).wait_recv()
        for d in range(2):
            go(x_copy(buf, ss, rs, 1, d, 0, yh_head))
        go(head_copy(buf, ss, rs, 10, yh_head, sib))

    def gather_near(buf, ss, rs, second):
        for d in range(2):
            slot = x_head(3 if d == 0 else 1, 1 - yh if second else yh, co)
            x_copy(buf, ss, rs, second, d, 0, slot).wait_recv()
            go(x_copy(buf, ss, rs, second, d, 1, slot))
            go(head_copy(buf, ss, rs, 11 + 2 * second + d, slot, sib))

    def gather_far(buf, ss, rs, second):
        slot = x_head(2, 1 - yh if second else yh, co)
        for d in range(2):
            x_copy(buf, ss, rs, second, d, 1, slot).wait_recv()
        go(head_copy(buf, ss, rs, 15 + second, slot, sib))

    def gather_end(buf, ss, rs):
        slots = [sib, x_head(0, 1 - yh, 1 - co)]
        for yh_ in (yh, 1 - yh):
            slots += [x_head(3, yh_, 1 - co), x_head(1, yh_, 1 - co)]
        slots += [x_head(2, yh_, 1 - co) for yh_ in (yh, 1 - yh)]
        for j, slot in enumerate(slots):
            head_copy(buf, ss, rs, 9 + j, slot, sib).wait_recv()

    def y_copy(index, src, dst):
        return remote(src, dst, y_ss.at[index], y_rs.at[index], y_dev)

    for t in range(2):
        for i in range(2):
            for d in range(2):
                go(kv_copy(d, 1, t, i))
    q_copy = y_copy(0, qs.at[0], qs.at[1])
    go(q_copy)
    gather_begin(cot_all, c_ss, c_rs)

    loads[4].wait()
    loads[5].wait()
    for i in range(2):
        kns[i] = in_order(kn, i)
        vns[i] = in_order(vn, i)
        knt[i] = kns[i].T
        vnt[i] = vns[i].T

    def transpose_slot(slot):
        for i in range(2):
            kt[slot, i] = kv[slot, 0, i].T
            vt[slot, i] = kv[slot, 1, i].T

    def get_state(qd, i):
        return ml[qd, i], ml[qd, 2 + i], acc[qd, i]

    def put_state(qd, i, state):
        ml[qd, i], ml[qd, 2 + i] = (jnp.broadcast_to(v, (8, BLOCK)) for v in state[:2])
        acc[qd, i] = state[2]

    def rows_of(state):
        return state[0][:1], state[1][:1], state[2]

    def seen_high(qd, slot):
        q_ctx = (yl + qd * (1 - 2 * yl)) * NZ + z
        return low_id(yl * NZ + slot) > low_id(q_ctx)

    def forward_pair(qd, slot):
        high = seen_high(qd, slot)
        q_low, q_high = qs[qd, 0], qs[qd, 1]
        state_high = forward_tile(
            kv[slot, 0, 0], vt[slot, 0], q_high, rows_of(get_state(qd, 1))
        )
        state_low = rows_of(get_state(qd, 0))
        state = tuple(jnp.where(high, a, b) for a, b in zip(state_high, state_low))
        state = forward_tile(
            jnp.where(high, kv[slot, 0, 1], kv[slot, 0, 0]),
            jnp.where(high, vt[slot, 1], vt[slot, 0]),
            jnp.where(high, q_high, q_low),
            state,
        )
        put_state(qd, 0, tuple(jnp.where(high, b, a) for a, b in zip(state, state_low)))
        put_state(qd, 1, tuple(jnp.where(high, a, b) for a, b in zip(state, state_high)))

    def w_across(j):
        columns = pl.ds(pl.multiple_of((j * 4 + (1 - yh) * 2) * 256, 512), 512)
        return remote(w.at[:, columns], w_mid.at[j], wm_ss.at[j], wm_rs.at[j], (c, yh_head))

    def send_w_across():
        loads[6].wait()
        for j in range(4):
            go(w_across(j))

    w_steps = [(1, 0), (1, 1), (3, 0), (3, 1), (2, 0), (2, 1), (0, 1)]

    def send_w(passed):
        if passed:
            for j in range(4):
                w_across(j).wait_recv()
        slot = yh_head if passed else h
        for j, (k, other) in enumerate(w_steps + [(0, 0)]):
            dest_core = (1 - co) if other else co
            if passed:
                columns = pl.ds(pl.multiple_of(dest_core * 256, 256), 256)
                src = w_mid.at[(x + k) % 4, :, columns]
            else:
                first = pl.multiple_of(head_of((x + k) % 4, yh, dest_core) * 256, 256)
                src = w.at[:, pl.ds(first, 256)]
            if j < 7:
                index = 7 * passed + j
                dev = (c, head_of((x + k) % 4, yh, dest_core))
                go(remote(src, w_cols.at[slot], w_ss.at[index], w_rs.at[index], dev))
            else:
                w_cols[slot] = src[...]

    def wait_w():
        for passed in range(2):
            for j, (k, other) in enumerate(w_steps):
                core = (1 - co) if other else co
                slot = head_of((x + 4 - k) % 4, 1 - yh if passed else yh, core)
                index = 7 * passed + j
                dev = (c, head_of((x + k) % 4, yh, core))
                here = w_cols.at[slot]
                remote(here, here, w_ss.at[index], w_rs.at[index], dev).wait_recv()

    def add_pieces(core, first):
        for i in range(2):
            rows = slice(i * BLOCK, (i + 1) * BLOCK)
            total = jnp.zeros((BLOCK, HEAD_DIM), F32) if first else do_acc[rows, :]
            for j in range(8):
                p = 2 * j + core
                columns = pl.ds(pl.multiple_of(p * 256, 256), 256)
                total = total + nt(cot_all[p, rows], w[:, columns])
            do_acc[rows, :] = total

    empty = (
        jnp.full((1, BLOCK), EMPTY, F32),
        jnp.zeros((1, BLOCK), F32),
        jnp.zeros((HEAD_DIM, BLOCK), F32),
    )
    transpose_slot(z)
    for i in range(2):
        state = forward_tile(kns[i], vnt[i], qs[0, i], empty)
        if i == 1:
            state = forward_tile(kv[z, 0, 0], vt[z, 0], qs[0, 1], state)
        put_state(0, i, state)
        put_state(1, i, empty)
    q_copy.wait_recv()
    forward_pair(1, z)

    for s in range(1, 5):
        for t in range(2):
            for i in range(2):
                for d in range(2):
                    if s < 4 or t == d:
                        kv_wait(d, s, t, i)
                        if s < 3 or (s == 3 and t == d):
                            go(kv_copy(d, s + 1, t, i))
        if s < 4:

            def step(i, carry, s=s):
                slot = (z + NZ + (2 * i - 1) * s) % NZ
                transpose_slot(slot)
                forward_pair(0, slot)
                forward_pair(1, slot)
                return carry

            lax.fori_loop(0, 2, step, 0)
        else:
            slot = (z + 4) % NZ
            transpose_slot(slot)
            forward_pair(1, slot)
            for i in range(2):
                acc_out[i] = acc[1, i].astype(BF)
            ml_copy = y_copy(1, ml.at[1], ml_in)
            acc_copy = y_copy(2, acc_out, acc_in)
            go(ml_copy)
            go(acc_copy)
            forward_pair(0, slot)
        if s == 1:
            gather_second(cot_all, c_ss, c_rs)
            send_w_across()
            gather_near(cot_all, c_ss, c_rs, 0)
        if s == 2:
            gather_far(cot_all, c_ss, c_rs, 0)
            gather_near(cot_all, c_ss, c_rs, 1)
        if s == 3:
            gather_far(cot_all, c_ss, c_rs, 1)
            send_w(0)
            add_pieces(co, True)

    gather_end(cot_all, c_ss, c_rs)
    add_pieces(1 - co, False)
    send_w(1)
    for i in range(2):
        dos[0, i] = do_acc[i * BLOCK : (i + 1) * BLOCK, :].astype(BF)
    do_copy = y_copy(3, dos.at[0], dos.at[1])
    go(do_copy)

    ml_copy.wait_recv()
    acc_copy.wait_recv()
    for i in range(2):
        own_max, own_sum, own_acc = rows_of(get_state(0, i))
        other_max, other_sum = ml_in[i][:1], ml_in[2 + i][:1]
        top = jnp.maximum(own_max, other_max)
        own_part = jnp.exp2((own_max - top) * SCALE2)
        other_part = jnp.exp2((other_max - top) * SCALE2)
        total = own_sum * own_part + other_sum * other_part
        weighted = own_acc * own_part + acc_in[i].astype(F32) * other_part
        attended_t = (weighted / total).astype(BF)
        att_t[:, i * BLOCK : (i + 1) * BLOCK] = attended_t
        att_all[h, i * BLOCK : (i + 1) * BLOCK, :] = attended_t.T
        grads_t = dos[0, i].T.astype(F32)
        row_dot = jnp.sum(grads_t * attended_t.astype(F32), axis=0, keepdims=True)
        ld[0, i] = jnp.broadcast_to(top * SCALE2 + jnp.log2(total), (8, BLOCK))
        ld[0, 2 + i] = jnp.broadcast_to(row_dot, (8, BLOCK))
    ld_copy = y_copy(4, ld.at[0], ld.at[1])
    go(ld_copy)
    gather_begin(att_all, a_ss, a_rs)

    def gy_slot(j):
        return (z + (4, 3, 5, 2, 6, 1, 7, 0)[j]) % NZ

    gy_copies = []

    def send_gy(first, last):
        for j in range(first, last):
            slot = gy_slot(j)
            gy_out[j] = nn(att_t[...], cot_all[(1 - yl) * NZ + slot]).astype(BF)
            gy_copies.append(remote(gy_out.at[j], gy_in.at[j], gy_ss.at[j], gy_rs.at[j], y_dev))
            go(gy_copies[-1])

    send_gy(0, 3)

    for i in range(2):
        key_term, value_term, query_term = backward_tile(
            kns[i], vns[i], knt[i], qs[0, i], dos[0, i], ld[0, i][:1], ld[0, 2 + i][:1]
        )
        stage[0, i] = (key_term * SCALE).astype(BF)
        stage[1, i] = value_term.astype(BF)
        dq[0, i] = query_term
        dq[1, i] = jnp.zeros_like(query_term)

    def unsort(index, out):
        for b in range(2):
            rows = jnp.where(swap, stage[index, 1 - b], stage[index, b])
            finals[index, b * BLOCK : (b + 1) * BLOCK, :] = rows
        put(finals.at[index], out)

    unsort(0, gkn)
    unsort(1, gvn)

    def backward_pair(d, qd, slot, same):
        low, high = (
            backward_tile(
                kv[slot, 0, 0], kv[slot, 1, 0], kt[slot, 0],
                qs[qd, 1], dos[qd, 1], ld[qd, 1][:1], ld[qd, 3][:1],
            ),
            None,
        )
        if same:
            cb[d, 0, 0] = low[0]
            cb[d, 1, 0] = low[1]
            cb[d, 0, 1] = jnp.zeros_like(low[0])
            cb[d, 1, 1] = jnp.zeros_like(low[1])
            dq[qd, 1] += low[2]
            return
        pick = seen_high(qd, slot)

        def chosen(first, second):
            return jnp.where(pick, second, first)

        high = backward_tile(
            chosen(kv[slot, 0, 0], kv[slot, 0, 1]),
            chosen(kv[slot, 1, 0], kv[slot, 1, 1]),
            chosen(kt[slot, 0], kt[slot, 1]),
            chosen(qs[qd, 0], qs[qd, 1]),
            chosen(dos[qd, 0], dos[qd, 1]),
            chosen(ld[qd, 0][:1], ld[qd, 1][:1]),
            chosen(ld[qd, 2][:1], ld[qd, 3][:1]),
        )
        to_high = pick.astype(F32)
        to_low = 1.0 - to_high
        for t in range(2):
            new_low = low[t] + high[t] * to_low
            new_high = high[t] * to_high
            if qd == 0:
                cb[d, t, 0] = new_low
                cb[d, t, 1] = new_high
            else:
                cb[d, t, 0] += new_low
                cb[d, t, 1] += new_high
        dq[qd, 0] += high[2] * to_low
        dq[qd, 1] += low[2] + high[2] * to_high

    def contributions(s):
        if s in (0, 4):
            slot = (z + 4 - s) % NZ
            backward_pair(0, 0, slot, s == 4)
            if s == 0:
                do_copy.wait_recv()
                ld_copy.wait_recv()
            backward_pair(0, 1, slot, False)
        else:

            def step(d, carry):
                slot = (z + NZ + (1 - 2 * d) * (4 - s)) % NZ
                backward_pair(d, 0, slot, False)
                backward_pair(d, 1, slot, False)
                return carry

            lax.fori_loop(0, 2, step, 0)

    factors = (SCALE, 1.0)

    def rs_copy(d, s, t, i):
        at = (d, s, t, i)
        return remote(rs_out.at[at], rs_in.at[at], r_ss.at[at], r_rs.at[at], z_dev[d])

    def g_copy(d, s):
        rows = pl.ds(64 * d, 64) if s == 0 else pl.ds(0, 128)
        return remote(
            g_out.at[d, s, rows], g_in.at[d, s, rows], g_ss.at[d, s], g_rs.at[d, s], z_dev[d]
        )

    def g_piece(j):
        gy_copies[j].wait_recv()
        own = nn(att_t[...], cot_all[yl * NZ + gy_slot(j)])
        return own + gy_in[j].astype(F32)

    contributions(0)
    for t in range(2):
        for i in range(2):
            rs_out[t, 0, t, i] = (cb[0, t, i] * factors[t]).astype(BF)
            go(rs_copy(t, 0, t, i))
    send_gy(3, 8)

    for s in range(1, 5):
        contributions(s)
        if s == 1:
            piece = g_piece(0).astype(BF)
            for d in range(2):
                g_out[d, 0] = piece
                go(g_copy(d, 0))
        else:
            for d in range(2):
                g_copy(d, s - 2).wait_recv()
                piece = g_piece(2 * (s - 1) - 1 + d)
                if s == 2:
                    half = slice(64 * d, 64 * d + 64)
                    rest = slice(64 - 64 * d, 128 - 64 * d)
                    g_out[d, 1, half] = (piece[half] + g_in[d, 0, half].astype(F32)).astype(BF)
                    g_out[d, 1, rest] = piece[rest].astype(BF)
                else:
                    g_out[d, s - 1] = (piece + g_in[d, s - 2].astype(F32)).astype(BF)
                go(g_copy(d, s - 1))
        if s < 4:
            for t, i, d in [(t, i, d) for t in range(2) for i in range(2) for d in range(2)]:
                term = cb[d, t, i] * factors[t]
                if s > 1 or t == d:
                    rs_copy(d, s - 1, t, i).wait_recv()
                    term = term + rs_in[d, s - 1, t, i].astype(F32)
                rs_out[d, s, t, i] = term.astype(BF)
                go(rs_copy(d, s, t, i))
        if s == 1:
            gather_second(att_all, a_ss, a_rs)
            gather_near(att_all, a_ss, a_rs, 0)
        if s == 2:
            gather_far(att_all, a_ss, a_rs, 0)
            gather_near(att_all, a_ss, a_rs, 1)
        if s == 3:
            gather_far(att_all, a_ss, a_rs, 1)

    for i in range(2):
        dq_out[i] = (dq[1, i] * SCALE).astype(BF)
    dq_copy = y_copy(5, dq_out, dq_in)
    go(dq_copy)

    gather_end(att_all, a_ss, a_rs)
    wait_w()
    total = nn(att_all[0], w_cols[0])
    for p in range(1, 16):
        total = total + nn(att_all[p], w_cols[p])
    cotm[...] = total.astype(BF)
    for b in range(2):
        mixed_final[b * BLOCK : (b + 1) * BLOCK, :] = in_order(cotm, b)
    put(mixed_final, mixed)

    dq_copy.wait_recv()
    for i in range(2):
        stage[2, i] = (dq[0, i] * SCALE + dq_in[i].astype(F32)).T.astype(BF)
    unsort(2, gq)

    piece = g_piece(7)
    for d in range(2):
        g_copy(d, 3).wait_recv()
        piece = piece + g_in[d, 3].astype(F32)
    gw_final[...] = piece
    put(gw_final, gw)

    for t in range(2):
        for i in range(2):
            for d in range(2):
                rs_copy(d, 3, t, i).wait_recv()
            stage[3 + t, i] = (
                cb[0, t, i] * factors[t]
                + rs_in[0, 3, t, i].astype(F32)
                + rs_in[1, 3, t, i].astype(F32)
            ).astype(BF)
        unsort(3 + t, (gkc, gvc)[t])

    for copy in sends:
        copy.wait_send()
    for store in stores:
        store.wait()


def hand_on(*refs):
    for i in range(7):
        refs[7 + i][...] = refs[i][...]


def per_device(q, kn, vn, kc, vc, w, cot, noise_mask, block_order):
    vmem = pl.BlockSpec(memory_space=pltpu.VMEM)
    smem = pl.BlockSpec(memory_space=pltpu.SMEM)
    rows, width = q.shape
    blk = (BLOCK, HEAD_DIM)
    tblk = (HEAD_DIM, BLOCK)
    dma = pltpu.SemaphoreType.DMA
    narrow = jax.ShapeDtypeStruct((rows, width), BF)
    scratch = [
        *[pltpu.VMEM((rows, width), BF)] * 5,
        pltpu.VMEM(w.shape, BF),
        pltpu.VMEM(cot.shape, BF),
        pltpu.VMEM((2, 2) + blk, BF),
        pltpu.VMEM((2,) + blk, BF),
        pltpu.VMEM((2,) + blk, BF),
        pltpu.VMEM((NZ, 2, 2) + blk, BF),
        pltpu.VMEM((NZ, 2) + tblk, BF),
        pltpu.VMEM((NZ, 2) + tblk, BF),
        pltpu.VMEM((2,) + tblk, BF),
        pltpu.VMEM((2,) + tblk, BF),
        pltpu.VMEM((2, 4, 8, BLOCK), F32),
        pltpu.VMEM((4, 8, BLOCK), F32),
        pltpu.VMEM((2, 2) + tblk, F32),
        pltpu.VMEM((2,) + tblk, BF),
        pltpu.VMEM((2,) + tblk, BF),
        pltpu.VMEM((rows, 256), BF),
        pltpu.VMEM((16, rows, 256), BF),
        pltpu.VMEM((16, HEAD_DIM, 256), BF),
        pltpu.VMEM((4, HEAD_DIM, 512), BF),
        pltpu.VMEM((HEAD_DIM, rows), BF),
        pltpu.VMEM((16, rows, HEAD_DIM), BF),
        pltpu.VMEM((rows, HEAD_DIM), F32),
        pltpu.VMEM((2, 2) + blk, BF),
        pltpu.VMEM((2, 4, 8, BLOCK), F32),
        pltpu.VMEM((2, 2) + tblk, F32),
        pltpu.VMEM((2,) + tblk, BF),
        pltpu.VMEM((2,) + tblk, BF),
        pltpu.VMEM((2, 2, 2) + blk, F32),
        pltpu.VMEM((2, 4, 2, 2) + blk, BF),
        pltpu.VMEM((2, 4, 2, 2) + blk, BF),
        pltpu.VMEM((8, HEAD_DIM, 256), BF),
        pltpu.VMEM((8, HEAD_DIM, 256), BF),
        pltpu.VMEM((2, 4, HEAD_DIM, 256), BF),
        pltpu.VMEM((2, 4, HEAD_DIM, 256), BF),
        pltpu.VMEM((5, 2) + blk, BF),
        pltpu.VMEM((5, rows, width), BF),
        pltpu.VMEM(cot.shape, BF),
        pltpu.VMEM((HEAD_DIM, 256), F32),
        dma((7,)), dma((7,)),
        dma((2, 4, 2, 2)), dma((2, 4, 2, 2)),
        dma((6,)), dma((6,)),
        dma((8,)), dma((8,)),
        dma((17,)), dma((17,)),
        dma((17,)), dma((17,)),
        dma((4,)), dma((4,)),
        dma((14,)), dma((14,)),
        dma((2, 4, 2, 2)), dma((2, 4, 2, 2)),
        dma((2, 4)), dma((2, 4)),
    ]
    shapes = (
        jax.ShapeDtypeStruct(cot.shape, BF),
        narrow, narrow, narrow, narrow, narrow,
        jax.ShapeDtypeStruct((HEAD_DIM, 256), F32),
    )
    anywhere = pl.BlockSpec(memory_space=pl.ANY)
    outs = pl.pallas_call(
        kernel,
        out_shape=shapes,
        in_specs=[smem, vmem] + [anywhere] * 7,
        out_specs=(anywhere,) * 7,
        scratch_shapes=scratch,
        compiler_params=pltpu.CompilerParams(
            collective_id=0, has_side_effects=True, vmem_limit_bytes=56 * 2**20
        ),
        name="block_attention",
    )(block_order, noise_mask.reshape(4, 128), q, kn, vn, kc, vc, w, cot)
    return pl.pallas_call(
        hand_on,
        out_shape=shapes,
        in_specs=[vmem] * 7,
        out_specs=(vmem,) * 7,
        name="hand_on",
    )(*outs)


def solution(mesh):
    spread = P("ctx", "head")
    return jax.shard_map(
        per_device,
        mesh=mesh,
        in_specs=(spread,) * 5 + (P("head", None), spread, P("ctx"), P()),
        out_specs=(spread,) * 6 + (P("head", "ctx"),),
        check_vma=False,
    )
```

```python
import functools

import jax
import jax.numpy as jnp
from jax import lax
from jax.experimental import pallas as pl
from jax.experimental.pallas import tpu as pltpu
from jax.sharding import PartitionSpec as P

BLOCK = 256
HEAD_DIM = 128
SCALE = HEAD_DIM**-0.5
SCALE2 = SCALE * 1.4426950408889634
EMPTY = -1e30
NZ = 8
MESH = pl.DeviceIdType.MESH
BF = jnp.bfloat16
F32 = jnp.float32


def nt(a, b):
    return lax.dot_general(a, b, (((1,), (1,)), ((), ())), preferred_element_type=F32)


def nn(a, b):
    return lax.dot_general(a, b, (((1,), (0,)), ((), ())), preferred_element_type=F32)


def remote(src, dst, send_sem, recv_sem, device):
    return pltpu.make_async_remote_copy(
        src_ref=src,
        dst_ref=dst,
        send_sem=send_sem,
        recv_sem=recv_sem,
        device_id=device,
        device_id_type=MESH,
    )


def forward_tile(keys, values_t, queries, state):
    row_max, row_sum, acc = state
    scores = nt(keys, queries)
    new_max = jnp.maximum(row_max, jnp.max(scores, axis=0, keepdims=True))
    weights = jnp.exp2((scores - new_max) * SCALE2)
    shrink = jnp.exp2((row_max - new_max) * SCALE2)
    new_sum = row_sum * shrink + jnp.sum(weights, axis=0, keepdims=True)
    new_acc = acc * shrink + nn(values_t, weights.astype(BF))
    return new_max, new_sum, new_acc


def backward_tile(keys, values, keys_t, queries, grads, log_total, row_dot):
    probs = jnp.exp2(nt(keys, queries) * SCALE2 - log_total)
    grad_probs = nt(values, grads)
    grad_scores = (probs * (grad_probs - row_dot)).astype(BF)
    return nn(grad_scores, queries), nn(probs.astype(BF), grads), nn(keys_t, grad_scores)


def kernel(
    order, mask, q_in, kn_in, vn_in, kc_in, vc_in, w_in, cot_in,
    mixed, gq, gkn, gvn, gkc, gvc, gw,
    q, kn, vn, kc, vc, w, cot,
    qs, kns, vns, kv, kt, vt, knt, vnt, ml, ml_in, acc, acc_out, acc_in,
    cotm, cot_all, w_cols, w_mid, att_t, att_all, do_acc, dos, ld, dq, dq_out, dq_in,
    cb, rs_out, rs_in, gy_out, gy_in, g_out, g_in, stage, finals, mixed_final, gw_final,
    in_sem, out_sem,
    kv_ss, kv_rs, y_ss, y_rs, gy_ss, gy_rs, c_ss, c_rs, a_ss, a_rs, wm_ss, wm_rs, w_ss, w_rs,
    r_ss, r_rs, g_ss, g_rs,
):
    c = lax.axis_index("ctx")
    h = lax.axis_index("head")
    yl, z = c // NZ, c % NZ
    x, yh, co = h // 4, (h // 2) % 2, h % 2
    sends = []

    def go(copy):
        copy.start()
        sends.append(copy)

    def head_of(x_, yh_, co_):
        return x_ * 4 + yh_ * 2 + co_

    z_dev = [(yl * NZ + (z + 1) % NZ, h), (yl * NZ + (z + NZ - 1) % NZ, h)]
    y_ctx = (1 - yl) * NZ + z
    y_dev = (y_ctx, h)
    heads = [head_of((x + k) % 4, yh, co_) for k in range(1, 4) for co_ in range(2)]
    heads += [head_of(x, yh, 1 - co), head_of(x, 1 - yh, co)]

    loads = [
        pltpu.make_async_copy(src, dst, in_sem.at[i])
        for i, (src, dst) in enumerate(
            ((kc_in, kc), (vc_in, vc), (cot_in, cot), (q_in, q), (kn_in, kn), (vn_in, vn), (w_in, w))
        )
    ]
    for load in loads:
        load.start()
    stores = []

    def put(src, dst):
        store = pltpu.make_async_copy(src, dst, out_sem.at[len(stores)])
        store.start()
        stores.append(store)

    barrier = pltpu.get_barrier_semaphore()
    for dev in z_dev + [y_dev] + [(c, p) for p in heads]:
        pl.semaphore_signal(barrier, inc=1, device_id=dev, device_id_type=MESH)

    swap = order[2 * c] > order[2 * c + 1]

    def in_order(ref, i):
        first, second = ref[:BLOCK, :], ref[BLOCK:, :]
        return jnp.where(swap, first, second) if i else jnp.where(swap, second, first)

    def low_id(ctx):
        return jnp.minimum(order[2 * ctx], order[2 * ctx + 1])

    loads[0].wait()
    loads[1].wait()
    for i in range(2):
        kv[z, 0, i] = in_order(kc, i)
        kv[z, 1, i] = in_order(vc, i)
    loads[2].wait()
    row_id = lax.broadcasted_iota(jnp.int32, (128, 128), 0)
    col_id = lax.broadcasted_iota(jnp.int32, (128, 128), 1)
    for b in range(4):
        flags = jnp.broadcast_to(mask[b : b + 1, :].astype(F32), (128, 128))
        column = jnp.sum(jnp.where(row_id == col_id, flags, 0.0), axis=1, keepdims=True)
        rows = slice(b * 128, (b + 1) * 128)
        cotm[rows, :] = (cot[rows, :].astype(F32) * column).astype(BF)
    for i in range(2):
        cot_all[h, i * BLOCK : (i + 1) * BLOCK, :] = in_order(cotm, i)

    loads[3].wait()
    for i in range(2):
        qs[0, i] = in_order(q, i)

    pl.semaphore_wait(barrier, 11)

    def kv_chunk(d, s, t, i, slot):
        chunk = kv.at[slot, t, i]
        return remote(chunk, chunk, kv_ss.at[d, s - 1, t, i], kv_rs.at[d, s - 1, t, i], z_dev[d])

    def kv_copy(d, s, t, i):
        return kv_chunk(d, s, t, i, (z + NZ - (s - 1)) % NZ if d == 0 else (z + s - 1) % NZ)

    def kv_wait(d, s, t, i):
        kv_chunk(d, s, t, i, (z + NZ - s) % NZ if d == 0 else (z + s) % NZ).wait_recv()

    def head_copy(buf, ss, rs, index, slot, dev_head):
        return remote(buf.at[slot], buf.at[slot], ss.at[index], rs.at[index], (c, dev_head))

    yh_head = head_of(x, 1 - yh, co)
    sib = head_of(x, yh, 1 - co)

    def x_head(k, yh_, co_):
        return head_of((x + k) % 4, yh_, co_)

    def rows_at(half):
        return pl.ds(BLOCK * half, BLOCK)

    def yh_copy(buf, ss, rs, half, slot):
        chunk = buf.at[slot, rows_at(half)]
        return remote(chunk, chunk, ss.at[half], rs.at[half], (c, yh_head))

    def x_copy(buf, ss, rs, second, d, kind, slot):
        index = 2 + 6 * second + 2 * kind + d
        chunk = buf.at[slot, rows_at(d if kind == 2 else kind)]
        dev = (c, x_head(1 if d == 0 else 3, yh, co))
        return remote(chunk, chunk, ss.at[index], rs.at[index], dev)

    def near_slot(second, d):
        return x_head(3 if d == 0 else 1, 1 - yh if second else yh, co)

    def gather_begin(buf, ss, rs, between=lambda: None):
        for half in range(2):
            go(yh_copy(buf, ss, rs, half, h))
            for d in range(2):
                go(x_copy(buf, ss, rs, 0, d, half, h))
            if half == 0:
                between()
        go(head_copy(buf, ss, rs, 14, h, sib))

    def gather_second(buf, ss, rs, half):
        yh_copy(buf, ss, rs, half, yh_head).wait_recv()
        for d in range(2):
            go(x_copy(buf, ss, rs, 1, d, half, yh_head))
        if half:
            go(head_copy(buf, ss, rs, 15, yh_head, sib))

    def gather_pass(buf, ss, rs, second, d):
        slot = near_slot(second, d)
        x_copy(buf, ss, rs, second, d, d, slot).wait_recv()
        go(x_copy(buf, ss, rs, second, d, 2, slot))

    def gather_near(buf, ss, rs, second):
        for d in range(2):
            slot = near_slot(second, d)
            x_copy(buf, ss, rs, second, d, 1 - d, slot).wait_recv()
            go(head_copy(buf, ss, rs, 16 + 2 * second + d, slot, sib))

    def gather_far(buf, ss, rs, second):
        slot = x_head(2, 1 - yh if second else yh, co)
        for d in range(2):
            x_copy(buf, ss, rs, second, d, 2, slot).wait_recv()
        go(head_copy(buf, ss, rs, 20 + second, slot, sib))

    def gather_end(buf, ss, rs):
        slots = [sib, x_head(0, 1 - yh, 1 - co)]
        for yh_ in (yh, 1 - yh):
            slots += [x_head(3, yh_, 1 - co), x_head(1, yh_, 1 - co)]
        slots += [x_head(2, yh_, 1 - co) for yh_ in (yh, 1 - yh)]
        for j, slot in enumerate(slots):
            head_copy(buf, ss, rs, 14 + j, slot, sib).wait_recv()

    def y_copy(index, src, dst):
        return remote(src, dst, y_ss.at[index], y_rs.at[index], y_dev)

    for t in range(2):
        for i in range(2):
            for d in range(2):
                go(kv_copy(d, 1, t, i))
    q_copy = y_copy(0, qs.at[0], qs.at[1])
    gather_begin(cot_all, c_ss, c_rs, lambda: go(q_copy))

    loads[4].wait()
    loads[5].wait()
    for i in range(2):
        kns[i] = in_order(kn, i)
        vns[i] = in_order(vn, i)
        knt[i] = kns[i].T
        vnt[i] = vns[i].T

    def transpose_slot(slot):
        for i in range(2):
            kt[slot, i] = kv[slot, 0, i].T
            vt[slot, i] = kv[slot, 1, i].T

    def get_state(qd, i):
        return ml[qd, i], ml[qd, 2 + i], acc[qd, i]

    def put_state(qd, i, state):
        ml[qd, i], ml[qd, 2 + i] = (jnp.broadcast_to(v, (8, BLOCK)) for v in state[:2])
        acc[qd, i] = state[2]

    def rows_of(state):
        return state[0][:1], state[1][:1], state[2]

    def seen_high(qd, slot):
        q_ctx = (yl + qd * (1 - 2 * yl)) * NZ + z
        return low_id(yl * NZ + slot) > low_id(q_ctx)

    def forward_pair(qd, slot):
        high = seen_high(qd, slot)
        q_low, q_high = qs[qd, 0], qs[qd, 1]
        state_high = forward_tile(
            kv[slot, 0, 0], vt[slot, 0], q_high, rows_of(get_state(qd, 1))
        )
        state_low = rows_of(get_state(qd, 0))
        state = tuple(jnp.where(high, a, b) for a, b in zip(state_high, state_low))
        state = forward_tile(
            jnp.where(high, kv[slot, 0, 1], kv[slot, 0, 0]),
            jnp.where(high, vt[slot, 1], vt[slot, 0]),
            jnp.where(high, q_high, q_low),
            state,
        )
        put_state(qd, 0, tuple(jnp.where(high, b, a) for a, b in zip(state, state_low)))
        put_state(qd, 1, tuple(jnp.where(high, a, b) for a, b in zip(state, state_high)))

    def w_across(j):
        columns = pl.ds(pl.multiple_of((j * 4 + (1 - yh) * 2) * 256, 512), 512)
        return remote(w.at[:, columns], w_mid.at[j], wm_ss.at[j], wm_rs.at[j], (c, yh_head))

    def send_w_across():
        loads[6].wait()
        for j in range(4):
            go(w_across(j))

    w_steps = [(1, 0), (1, 1), (3, 0), (3, 1), (2, 0), (2, 1), (0, 1)]

    def send_w(passed):
        if passed:
            for j in range(4):
                w_across(j).wait_recv()
        slot = yh_head if passed else h
        for j, (k, other) in enumerate(w_steps + [(0, 0)]):
            dest_core = (1 - co) if other else co
            if passed:
                columns = pl.ds(pl.multiple_of(dest_core * 256, 256), 256)
                src = w_mid.at[(x + k) % 4, :, columns]
            else:
                first = pl.multiple_of(head_of((x + k) % 4, yh, dest_core) * 256, 256)
                src = w.at[:, pl.ds(first, 256)]
            if j < 7:
                index = 7 * passed + j
                dev = (c, head_of((x + k) % 4, yh, dest_core))
                go(remote(src, w_cols.at[slot], w_ss.at[index], w_rs.at[index], dev))
            else:
                w_cols[slot] = src[...]

    def wait_w():
        for passed in range(2):
            for j, (k, other) in enumerate(w_steps):
                core = (1 - co) if other else co
                slot = head_of((x + 4 - k) % 4, 1 - yh if passed else yh, core)
                index = 7 * passed + j
                dev = (c, head_of((x + k) % 4, yh, core))
                here = w_cols.at[slot]
                remote(here, here, w_ss.at[index], w_rs.at[index], dev).wait_recv()

    def add_pieces(core, first):
        for i in range(2):
            rows = slice(i * BLOCK, (i + 1) * BLOCK)
            total = jnp.zeros((BLOCK, HEAD_DIM), F32) if first else do_acc[rows, :]
            for j in range(8):
                p = 2 * j + core
                columns = pl.ds(pl.multiple_of(p * 256, 256), 256)
                total = total + nt(cot_all[p, rows], w[:, columns])
            do_acc[rows, :] = total

    empty = (
        jnp.full((1, BLOCK), EMPTY, F32),
        jnp.zeros((1, BLOCK), F32),
        jnp.zeros((HEAD_DIM, BLOCK), F32),
    )
    transpose_slot(z)
    for i in range(2):
        state = forward_tile(kns[i], vnt[i], qs[0, i], empty)
        if i == 1:
            state = forward_tile(kv[z, 0, 0], vt[z, 0], qs[0, 1], state)
        put_state(0, i, state)
        put_state(1, i, empty)
    def slot_tasks(slot):
        def first():
            transpose_slot(slot)
            forward_pair(0, slot)

        return [first, lambda: forward_pair(1, slot)]

    def late_queries():
        q_copy.wait_recv()
        forward_pair(1, z)

    cot_args = (cot_all, c_ss, c_rs)
    hooks = {
        (1, 2): lambda: gather_second(*cot_args, 0),
        (1, 3): lambda: [gather_pass(*cot_args, 0, d) for d in range(2)],
        (2, 1): lambda: [gather_second(*cot_args, 1), gather_near(*cot_args, 0)],
        (2, 2): lambda: gather_pass(*cot_args, 1, 0),
        (2, 3): lambda: send_w_across(),
        (3, 0): lambda: gather_far(*cot_args, 0),
        (3, 1): lambda: gather_pass(*cot_args, 1, 1),
        (3, 3): lambda: gather_near(*cot_args, 1),
    }
    tasks = []
    for s in range(1, 5):
        events = [(t, i) for t in range(2) for i in range(2)]
        if s == 4:
            events = [(t, i) for i in range(2) for t in range(2)]
        for n, (t, i) in enumerate(events):
            for d in range(2):
                if s < 4 or t == d:
                    kv_wait(d, s, t, i)
                    if s < 3 or (s == 3 and t == d):
                        go(kv_copy(d, s + 1, t, i))
            if (s, n) in hooks:
                hooks[s, n]()
            if tasks:
                tasks.pop(0)()
        if s == 1:
            tasks.append(late_queries)
        if s < 4:
            tasks += slot_tasks((z + NZ - s) % NZ) + slot_tasks((z + s) % NZ)
    while tasks:
        tasks.pop(0)()
    slot = (z + 4) % NZ
    transpose_slot(slot)
    forward_pair(1, slot)
    for i in range(2):
        acc_out[i] = acc[1, i].astype(BF)
    ml_copy = y_copy(1, ml.at[1], ml_in)
    acc_copy = y_copy(2, acc_out, acc_in)
    go(ml_copy)
    go(acc_copy)
    gather_far(*cot_args, 1)
    add_pieces(co, True)
    gather_end(*cot_args)
    add_pieces(1 - co, False)
    for i in range(2):
        dos[0, i] = do_acc[i * BLOCK : (i + 1) * BLOCK, :].astype(BF)
    do_copy = y_copy(3, dos.at[0], dos.at[1])
    go(do_copy)
    forward_pair(0, (z + 4) % NZ)
    send_w(0)

    ml_copy.wait_recv()
    acc_copy.wait_recv()
    for i in range(2):
        own_max, own_sum, own_acc = rows_of(get_state(0, i))
        other_max, other_sum = ml_in[i][:1], ml_in[2 + i][:1]
        top = jnp.maximum(own_max, other_max)
        own_part = jnp.exp2((own_max - top) * SCALE2)
        other_part = jnp.exp2((other_max - top) * SCALE2)
        total = own_sum * own_part + other_sum * other_part
        weighted = own_acc * own_part + acc_in[i].astype(F32) * other_part
        attended_t = (weighted / total).astype(BF)
        att_t[:, i * BLOCK : (i + 1) * BLOCK] = attended_t
        att_all[h, i * BLOCK : (i + 1) * BLOCK, :] = attended_t.T
        grads_t = dos[0, i].T.astype(F32)
        row_dot = jnp.sum(grads_t * attended_t.astype(F32), axis=0, keepdims=True)
        ld[0, i] = jnp.broadcast_to(top * SCALE2 + jnp.log2(total), (8, BLOCK))
        ld[0, 2 + i] = jnp.broadcast_to(row_dot, (8, BLOCK))
    ld_copy = y_copy(4, ld.at[0], ld.at[1])
    go(ld_copy)
    gather_begin(att_all, a_ss, a_rs)

    def gy_slot(j):
        return (z + (4, 3, 5, 2, 6, 1, 7, 0)[j]) % NZ

    gy_copies = []

    def send_gy(first, last):
        for j in range(first, last):
            slot = gy_slot(j)
            gy_out[j] = nn(att_t[...], cot_all[(1 - yl) * NZ + slot]).astype(BF)
            gy_copies.append(remote(gy_out.at[j], gy_in.at[j], gy_ss.at[j], gy_rs.at[j], y_dev))
            go(gy_copies[-1])

    send_gy(0, 3)

    for i in range(2):
        key_term, value_term, query_term = backward_tile(
            kns[i], vns[i], knt[i], qs[0, i], dos[0, i], ld[0, i][:1], ld[0, 2 + i][:1]
        )
        stage[0, i] = (key_term * SCALE).astype(BF)
        stage[1, i] = value_term.astype(BF)
        dq[0, i] = query_term
        dq[1, i] = jnp.zeros_like(query_term)

    def unsort(index, out):
        for b in range(2):
            rows = jnp.where(swap, stage[index, 1 - b], stage[index, b])
            finals[index, b * BLOCK : (b + 1) * BLOCK, :] = rows
        put(finals.at[index], out)

    unsort(0, gkn)
    unsort(1, gvn)

    def backward_pair(par, d, qd, slot, same=False):
        low, high = (
            backward_tile(
                kv[slot, 0, 0], kv[slot, 1, 0], kt[slot, 0],
                qs[qd, 1], dos[qd, 1], ld[qd, 1][:1], ld[qd, 3][:1],
            ),
            None,
        )
        if same:
            cb[par, d, 0, 0] = low[0]
            cb[par, d, 1, 0] = low[1]
            cb[par, d, 0, 1] = jnp.zeros_like(low[0])
            cb[par, d, 1, 1] = jnp.zeros_like(low[1])
            dq[qd, 1] += low[2]
            return
        pick = seen_high(qd, slot)

        def chosen(first, second):
            return jnp.where(pick, second, first)

        high = backward_tile(
            chosen(kv[slot, 0, 0], kv[slot, 0, 1]),
            chosen(kv[slot, 1, 0], kv[slot, 1, 1]),
            chosen(kt[slot, 0], kt[slot, 1]),
            chosen(qs[qd, 0], qs[qd, 1]),
            chosen(dos[qd, 0], dos[qd, 1]),
            chosen(ld[qd, 0][:1], ld[qd, 1][:1]),
            chosen(ld[qd, 2][:1], ld[qd, 3][:1]),
        )
        to_high = pick.astype(F32)
        to_low = 1.0 - to_high
        for t in range(2):
            new_low = low[t] + high[t] * to_low
            new_high = high[t] * to_high
            if qd == 0:
                cb[par, d, t, 0] = new_low
                cb[par, d, t, 1] = new_high
            else:
                cb[par, d, t, 0] += new_low
                cb[par, d, t, 1] += new_high
        dq[qd, 0] += high[2] * to_low
        dq[qd, 1] += low[2] + high[2] * to_high

    def contribution_tasks(s):
        par = s % 2
        if s in (0, 4):
            slot = (z + 4 - s) % NZ
            pairs = [(0, 0, slot, s == 4), (0, 1, slot)]
        else:
            slots = [(z + 4 - s) % NZ, (z + NZ - 4 + s) % NZ]
            pairs = [(d, qd, slots[d]) for d in range(2) for qd in range(2)]
        return [functools.partial(backward_pair, par, *pair) for pair in pairs]

    factors = (SCALE, 1.0)

    def rs_copy(d, s, t, i):
        at = (d, s, t, i)
        return remote(rs_out.at[at], rs_in.at[at], r_ss.at[at], r_rs.at[at], z_dev[d])

    def g_copy(d, s):
        rows = pl.ds(64 * d, 64) if s == 0 else pl.ds(0, 128)
        return remote(
            g_out.at[d, s, rows], g_in.at[d, s, rows], g_ss.at[d, s], g_rs.at[d, s], z_dev[d]
        )

    def g_piece(j):
        gy_copies[j].wait_recv()
        own = nn(att_t[...], cot_all[yl * NZ + gy_slot(j)])
        return own + gy_in[j].astype(F32)

    own, other = contribution_tasks(0)
    own()
    do_copy.wait_recv()
    ld_copy.wait_recv()
    other()
    for t in range(2):
        for i in range(2):
            rs_out[t, 0, t, i] = (cb[0, 0, t, i] * factors[t]).astype(BF)
            go(rs_copy(t, 0, t, i))
    send_gy(3, 8)
    send_w(1)

    def rs_step(s, tasks):
        for t, i, d in [(t, i, d) for t in range(2) for i in range(2) for d in range(2)]:
            term = cb[s % 2, d, t, i] * factors[t]
            if s > 1 or t == d:
                rs_copy(d, s - 1, t, i).wait_recv()
                term = term + rs_in[d, s - 1, t, i].astype(F32)
            rs_out[d, s, t, i] = term.astype(BF)
            go(rs_copy(d, s, t, i))
            if d and tasks:
                tasks.pop(0)()

    def g_step(s):
        if s == 0:
            piece = g_piece(0).astype(BF)
            for d in range(2):
                g_out[d, 0] = piece
                go(g_copy(d, 0))
            return
        for d in range(2):
            piece = g_piece(2 * s - 1 + d)
            g_copy(d, s - 1).wait_recv()
            if s == 1:
                half = slice(64 * d, 64 * d + 64)
                rest = slice(64 - 64 * d, 128 - 64 * d)
                g_out[d, 1, half] = (piece[half] + g_in[d, 0, half].astype(F32)).astype(BF)
                g_out[d, 1, rest] = piece[rest].astype(BF)
            else:
                g_out[d, s] = (piece + g_in[d, s - 1].astype(F32)).astype(BF)
            go(g_copy(d, s))

    for task in contribution_tasks(1):
        task()
    g_step(0)
    rs_step(1, contribution_tasks(2))
    g_step(1)
    gather_second(att_all, a_ss, a_rs, 0)
    gather_second(att_all, a_ss, a_rs, 1)
    gather_pass(att_all, a_ss, a_rs, 0, 0)
    gather_pass(att_all, a_ss, a_rs, 0, 1)
    gather_near(att_all, a_ss, a_rs, 0)
    rs_step(2, contribution_tasks(3))
    g_step(2)
    gather_pass(att_all, a_ss, a_rs, 1, 0)
    gather_pass(att_all, a_ss, a_rs, 1, 1)
    gather_near(att_all, a_ss, a_rs, 1)
    gather_far(att_all, a_ss, a_rs, 0)
    older = len(sends)
    rs_step(3, contribution_tasks(4))
    g_step(3)
    gather_far(att_all, a_ss, a_rs, 1)
    for copy in sends[:older]:
        copy.wait_send()
    del sends[:older]

    for i in range(2):
        dq_out[i] = (dq[1, i] * SCALE).astype(BF)
    dq_copy = y_copy(5, dq_out, dq_in)
    go(dq_copy)

    gather_end(att_all, a_ss, a_rs)
    wait_w()
    total = nn(att_all[0], w_cols[0])
    for p in range(1, 16):
        total = total + nn(att_all[p], w_cols[p])
    cotm[...] = total.astype(BF)
    for b in range(2):
        mixed_final[b * BLOCK : (b + 1) * BLOCK, :] = in_order(cotm, b)
    put(mixed_final, mixed)

    dq_copy.wait_recv()
    for i in range(2):
        stage[2, i] = (dq[0, i] * SCALE + dq_in[i].astype(F32)).T.astype(BF)
    unsort(2, gq)

    piece = g_piece(7)
    for d in range(2):
        g_copy(d, 3).wait_recv()
        piece = piece + g_in[d, 3].astype(F32)
    gw_final[...] = piece
    put(gw_final, gw)

    for t in range(2):
        for i in range(2):
            for d in range(2):
                rs_copy(d, 3, t, i).wait_recv()
            stage[3 + t, i] = (
                cb[0, 0, t, i] * factors[t]
                + rs_in[0, 3, t, i].astype(F32)
                + rs_in[1, 3, t, i].astype(F32)
            ).astype(BF)
        unsort(3 + t, (gkc, gvc)[t])

    for copy in sends:
        copy.wait_send()
    for store in stores:
        store.wait()


def hand_on(*refs):
    for i in range(7):
        refs[7 + i][...] = refs[i][...]


def per_device(q, kn, vn, kc, vc, w, cot, noise_mask, block_order):
    vmem = pl.BlockSpec(memory_space=pltpu.VMEM)
    smem = pl.BlockSpec(memory_space=pltpu.SMEM)
    rows, width = q.shape
    blk = (BLOCK, HEAD_DIM)
    tblk = (HEAD_DIM, BLOCK)
    dma = pltpu.SemaphoreType.DMA
    narrow = jax.ShapeDtypeStruct((rows, width), BF)
    scratch = [
        *[pltpu.VMEM((rows, width), BF)] * 5,
        pltpu.VMEM(w.shape, BF),
        pltpu.VMEM(cot.shape, BF),
        pltpu.VMEM((2, 2) + blk, BF),
        pltpu.VMEM((2,) + blk, BF),
        pltpu.VMEM((2,) + blk, BF),
        pltpu.VMEM((NZ, 2, 2) + blk, BF),
        pltpu.VMEM((NZ, 2) + tblk, BF),
        pltpu.VMEM((NZ, 2) + tblk, BF),
        pltpu.VMEM((2,) + tblk, BF),
        pltpu.VMEM((2,) + tblk, BF),
        pltpu.VMEM((2, 4, 8, BLOCK), F32),
        pltpu.VMEM((4, 8, BLOCK), F32),
        pltpu.VMEM((2, 2) + tblk, F32),
        pltpu.VMEM((2,) + tblk, BF),
        pltpu.VMEM((2,) + tblk, BF),
        pltpu.VMEM((rows, 256), BF),
        pltpu.VMEM((16, rows, 256), BF),
        pltpu.VMEM((16, HEAD_DIM, 256), BF),
        pltpu.VMEM((4, HEAD_DIM, 512), BF),
        pltpu.VMEM((HEAD_DIM, rows), BF),
        pltpu.VMEM((16, rows, HEAD_DIM), BF),
        pltpu.VMEM((rows, HEAD_DIM), F32),
        pltpu.VMEM((2, 2) + blk, BF),
        pltpu.VMEM((2, 4, 8, BLOCK), F32),
        pltpu.VMEM((2, 2) + tblk, F32),
        pltpu.VMEM((2,) + tblk, BF),
        pltpu.VMEM((2,) + tblk, BF),
        pltpu.VMEM((2, 2, 2, 2) + blk, F32),
        pltpu.VMEM((2, 4, 2, 2) + blk, BF),
        pltpu.VMEM((2, 4, 2, 2) + blk, BF),
        pltpu.VMEM((8, HEAD_DIM, 256), BF),
        pltpu.VMEM((8, HEAD_DIM, 256), BF),
        pltpu.VMEM((2, 4, HEAD_DIM, 256), BF),
        pltpu.VMEM((2, 4, HEAD_DIM, 256), BF),
        pltpu.VMEM((5, 2) + blk, BF),
        pltpu.VMEM((5, rows, width), BF),
        pltpu.VMEM(cot.shape, BF),
        pltpu.VMEM((HEAD_DIM, 256), F32),
        dma((7,)), dma((7,)),
        dma((2, 4, 2, 2)), dma((2, 4, 2, 2)),
        dma((6,)), dma((6,)),
        dma((8,)), dma((8,)),
        dma((22,)), dma((22,)),
        dma((22,)), dma((22,)),
        dma((4,)), dma((4,)),
        dma((14,)), dma((14,)),
        dma((2, 4, 2, 2)), dma((2, 4, 2, 2)),
        dma((2, 4)), dma((2, 4)),
    ]
    shapes = (
        jax.ShapeDtypeStruct(cot.shape, BF),
        narrow, narrow, narrow, narrow, narrow,
        jax.ShapeDtypeStruct((HEAD_DIM, 256), F32),
    )

    outs = pl.pallas_call(
        kernel,
        out_shape=tuple(pltpu.VMEM(shape.shape, shape.dtype) for shape in shapes),
        in_specs=[smem, vmem] + [pl.BlockSpec(memory_space=pltpu.HBM)] * 7,
        scratch_shapes=scratch,
        compiler_params=pltpu.CompilerParams(
            collective_id=0, has_side_effects=True, vmem_limit_bytes=56 * 2**20
        ),
        name="block_attention",
    )(block_order, noise_mask.reshape(4, 128), q, kn, vn, kc, vc, w, cot)
    return pl.pallas_call(
        hand_on,
        out_shape=shapes,
        in_specs=[vmem] * 7,
        out_specs=(vmem,) * 7,
        compiler_params=pltpu.CompilerParams(vmem_limit_bytes=8 * 2**20),
        name="hand_on",
    )(*outs)


def solution(mesh):
    spread = P("ctx", "head")
    return jax.shard_map(
        per_device,
        mesh=mesh,
        in_specs=(spread,) * 5 + (P("head", None), spread, P("ctx"), P()),
        out_specs=(spread,) * 6 + (P("head", "ctx"),),
        check_vma=False,
    )
```

```python
import functools

import jax
import jax.numpy as jnp
from jax import lax
from jax.experimental import pallas as pl
from jax.experimental.pallas import tpu as pltpu
from jax.sharding import PartitionSpec as P

BLOCK = 256
HEAD_DIM = 128
SCALE = HEAD_DIM**-0.5
SCALE2 = SCALE * 1.4426950408889634
EMPTY = -1e30
NZ = 8
MESH = pl.DeviceIdType.MESH
BF = jnp.bfloat16
F32 = jnp.float32


def nt(a, b):
    return lax.dot_general(a, b, (((1,), (1,)), ((), ())), preferred_element_type=F32)


def nn(a, b):
    return lax.dot_general(a, b, (((1,), (0,)), ((), ())), preferred_element_type=F32)


def remote(src, dst, send_sem, recv_sem, device):
    return pltpu.make_async_remote_copy(
        src_ref=src,
        dst_ref=dst,
        send_sem=send_sem,
        recv_sem=recv_sem,
        device_id=device,
        device_id_type=MESH,
    )


def forward_tile(keys, values_t, queries, state):
    row_max, row_sum, acc = state
    scores = nt(keys, queries)
    new_max = jnp.maximum(row_max, jnp.max(scores, axis=0, keepdims=True))
    weights = jnp.exp2((scores - new_max) * SCALE2)
    shrink = jnp.exp2((row_max - new_max) * SCALE2)
    new_sum = row_sum * shrink + jnp.sum(weights, axis=0, keepdims=True)
    new_acc = acc * shrink + nn(values_t, weights.astype(BF))
    return new_max, new_sum, new_acc


def backward_tile(keys, values, keys_t, queries, grads, log_total, row_dot):
    probs = jnp.exp2(nt(keys, queries) * SCALE2 - log_total)
    grad_probs = nt(values, grads)
    grad_scores = (probs * (grad_probs - row_dot)).astype(BF)
    return nn(grad_scores, queries), nn(probs.astype(BF), grads), nn(keys_t, grad_scores)


def kernel(
    order, mask, q_in, kn_in, vn_in, kc_in, vc_in, w_in, cot_in,
    mixed, gq, gkn, gvn, gkc, gvc, gw,
    q, kn, vn, kc, vc, w, cot,
    qs, kns, vns, kv, kt, vt, knt, vnt, ml, ml_in, acc, acc_out, acc_in,
    cotm, cot_all, w_cols, w_mid, att_t, att_all, do_acc, dos, dos_t, ld, dq, dq_out, dq_in,
    cb, rs_out, rs_in, gy_out, gy_in, g_out, g_in, stage, finals, mixed_final, gw_final,
    in_sem, out_sem,
    kv_ss, kv_rs, y_ss, y_rs, gy_ss, gy_rs, c_ss, c_rs, a_ss, a_rs, wm_ss, wm_rs, w_ss, w_rs,
    r_ss, r_rs, g_ss, g_rs,
):
    c = lax.axis_index("ctx")
    h = lax.axis_index("head")
    yl, z = c // NZ, c % NZ
    x, yh, co = h // 4, (h // 2) % 2, h % 2
    sends = []

    def go(copy):
        copy.start()
        sends.append(copy)

    def head_of(x_, yh_, co_):
        return x_ * 4 + yh_ * 2 + co_

    z_dev = [(yl * NZ + (z + 1) % NZ, h), (yl * NZ + (z + NZ - 1) % NZ, h)]
    y_ctx = (1 - yl) * NZ + z
    y_dev = (y_ctx, h)
    heads = [head_of((x + k) % 4, yh, co_) for k in range(1, 4) for co_ in range(2)]
    heads += [head_of(x, yh, 1 - co), head_of(x, 1 - yh, co)]

    loads = [
        pltpu.make_async_copy(src, dst, in_sem.at[i])
        for i, (src, dst) in enumerate(
            ((kc_in, kc), (vc_in, vc), (cot_in, cot), (q_in, q), (kn_in, kn), (vn_in, vn), (w_in, w))
        )
    ]
    for load in loads:
        load.start()
    stores = []

    def put(src, dst):
        store = pltpu.make_async_copy(src, dst, out_sem.at[len(stores)])
        store.start()
        stores.append(store)

    barrier = pltpu.get_barrier_semaphore()
    for dev in z_dev + [y_dev] + [(c, p) for p in heads]:
        pl.semaphore_signal(barrier, inc=1, device_id=dev, device_id_type=MESH)

    swap = order[2 * c] > order[2 * c + 1]

    def in_order(ref, i):
        first, second = ref[:BLOCK, :], ref[BLOCK:, :]
        return jnp.where(swap, first, second) if i else jnp.where(swap, second, first)

    def low_id(ctx):
        return jnp.minimum(order[2 * ctx], order[2 * ctx + 1])

    loads[0].wait()
    loads[1].wait()
    for i in range(2):
        kv[z, 0, i] = in_order(kc, i)
        kv[z, 1, i] = in_order(vc, i)
    pl.semaphore_wait(barrier, 11)

    def kv_chunk(d, s, t, i, slot):
        chunk = kv.at[slot, t, i]
        return remote(chunk, chunk, kv_ss.at[d, s - 1, t, i], kv_rs.at[d, s - 1, t, i], z_dev[d])

    def kv_copy(d, s, t, i):
        return kv_chunk(d, s, t, i, (z + NZ - (s - 1)) % NZ if d == 0 else (z + s - 1) % NZ)

    def kv_wait(d, s, t, i):
        kv_chunk(d, s, t, i, (z + NZ - s) % NZ if d == 0 else (z + s) % NZ).wait_recv()

    def head_copy(buf, ss, rs, index, slot, dev_head):
        return remote(buf.at[slot], buf.at[slot], ss.at[index], rs.at[index], (c, dev_head))

    yh_head = head_of(x, 1 - yh, co)
    sib = head_of(x, yh, 1 - co)

    def x_head(k, yh_, co_):
        return head_of((x + k) % 4, yh_, co_)

    def rows_at(half):
        return pl.ds(BLOCK * half, BLOCK)

    def yh_copy(buf, ss, rs, half, slot):
        chunk = buf.at[slot, rows_at(half)]
        return remote(chunk, chunk, ss.at[half], rs.at[half], (c, yh_head))

    def x_copy(buf, ss, rs, second, d, kind, slot):
        index = 2 + 6 * second + 2 * kind + d
        chunk = buf.at[slot, rows_at(d if kind == 2 else kind)]
        dev = (c, x_head(1 if d == 0 else 3, yh, co))
        return remote(chunk, chunk, ss.at[index], rs.at[index], dev)

    def near_slot(second, d):
        return x_head(3 if d == 0 else 1, 1 - yh if second else yh, co)

    def gather_begin(buf, ss, rs, between=lambda: None):
        for half in range(2):
            go(yh_copy(buf, ss, rs, half, h))
            for d in range(2):
                go(x_copy(buf, ss, rs, 0, d, half, h))
            if half == 0:
                between()
        go(head_copy(buf, ss, rs, 14, h, sib))

    def gather_second(buf, ss, rs, half):
        yh_copy(buf, ss, rs, half, yh_head).wait_recv()
        for d in range(2):
            go(x_copy(buf, ss, rs, 1, d, half, yh_head))
        if half:
            go(head_copy(buf, ss, rs, 15, yh_head, sib))

    def gather_pass(buf, ss, rs, second, d):
        slot = near_slot(second, d)
        x_copy(buf, ss, rs, second, d, d, slot).wait_recv()
        go(x_copy(buf, ss, rs, second, d, 2, slot))

    def gather_near(buf, ss, rs, second):
        for d in range(2):
            slot = near_slot(second, d)
            x_copy(buf, ss, rs, second, d, 1 - d, slot).wait_recv()
            go(head_copy(buf, ss, rs, 16 + 2 * second + d, slot, sib))

    def gather_far(buf, ss, rs, second):
        slot = x_head(2, 1 - yh if second else yh, co)
        for d in range(2):
            x_copy(buf, ss, rs, second, d, 2, slot).wait_recv()
        go(head_copy(buf, ss, rs, 20 + second, slot, sib))

    sib_slots = [sib, x_head(0, 1 - yh, 1 - co)]
    for yh_ in (yh, 1 - yh):
        sib_slots += [x_head(3, yh_, 1 - co), x_head(1, yh_, 1 - co)]
    sib_slots += [x_head(2, yh_, 1 - co) for yh_ in (yh, 1 - yh)]

    def gather_end(buf, ss, rs, first=0, last=8):
        for j in range(first, last):
            head_copy(buf, ss, rs, 14 + j, sib_slots[j], sib).wait_recv()

    def y_copy(index, src, dst):
        return remote(src, dst, y_ss.at[index], y_rs.at[index], y_dev)

    for t in range(2):
        for i in range(2):
            for d in range(2):
                go(kv_copy(d, 1, t, i))

    loads[2].wait()
    row_id = lax.broadcasted_iota(jnp.int32, (128, 128), 0)
    col_id = lax.broadcasted_iota(jnp.int32, (128, 128), 1)
    for b in range(4):
        flags = jnp.broadcast_to(mask[b : b + 1, :].astype(F32), (128, 128))
        column = jnp.sum(jnp.where(row_id == col_id, flags, 0.0), axis=1, keepdims=True)
        rows = slice(b * 128, (b + 1) * 128)
        cotm[rows, :] = (cot[rows, :].astype(F32) * column).astype(BF)
    for i in range(2):
        cot_all[h, i * BLOCK : (i + 1) * BLOCK, :] = in_order(cotm, i)

    loads[3].wait()
    for i in range(2):
        qs[0, i] = in_order(q, i)
    q_copy = y_copy(0, qs.at[0], qs.at[1])
    gather_begin(cot_all, c_ss, c_rs, lambda: go(q_copy))

    loads[4].wait()
    loads[5].wait()
    for i in range(2):
        kns[i] = in_order(kn, i)
        vns[i] = in_order(vn, i)
        knt[i] = kns[i].T
        vnt[i] = vns[i].T

    def transpose_slot(slot):
        for i in range(2):
            kt[slot, i] = kv[slot, 0, i].T
            vt[slot, i] = kv[slot, 1, i].T

    def get_state(qd, i):
        return ml[qd, i], ml[qd, 2 + i], acc[qd, i]

    def put_state(qd, i, state):
        ml[qd, i], ml[qd, 2 + i] = (jnp.broadcast_to(v, (8, BLOCK)) for v in state[:2])
        acc[qd, i] = state[2]

    def rows_of(state):
        return state[0][:1], state[1][:1], state[2]

    def seen_high(qd, slot):
        q_ctx = (yl + qd * (1 - 2 * yl)) * NZ + z
        return low_id(yl * NZ + slot) > low_id(q_ctx)

    def forward_pair(qd, slot):
        high = seen_high(qd, slot)
        q_low, q_high = qs[qd, 0], qs[qd, 1]
        state_high = forward_tile(
            kv[slot, 0, 0], vt[slot, 0], q_high, rows_of(get_state(qd, 1))
        )
        state_low = rows_of(get_state(qd, 0))
        state = tuple(jnp.where(high, a, b) for a, b in zip(state_high, state_low))
        state = forward_tile(
            jnp.where(high, kv[slot, 0, 1], kv[slot, 0, 0]),
            jnp.where(high, vt[slot, 1], vt[slot, 0]),
            jnp.where(high, q_high, q_low),
            state,
        )
        put_state(qd, 0, tuple(jnp.where(high, b, a) for a, b in zip(state, state_low)))
        put_state(qd, 1, tuple(jnp.where(high, a, b) for a, b in zip(state, state_high)))

    def w_across(j):
        columns = pl.ds(pl.multiple_of((j * 4 + (1 - yh) * 2) * 256, 512), 512)
        return remote(w.at[:, columns], w_mid.at[j], wm_ss.at[j], wm_rs.at[j], (c, yh_head))

    def send_w_across():
        loads[6].wait()
        for j in range(4):
            go(w_across(j))

    w_steps = [(1, 0), (1, 1), (3, 0), (3, 1), (2, 0), (2, 1), (0, 1)]

    def send_w(passed):
        if passed:
            for j in range(4):
                w_across(j).wait_recv()
        slot = yh_head if passed else h
        for j, (k, other) in enumerate(w_steps + [(0, 0)]):
            dest_core = (1 - co) if other else co
            if passed:
                columns = pl.ds(pl.multiple_of(dest_core * 256, 256), 256)
                src = w_mid.at[(x + k) % 4, :, columns]
            else:
                first = pl.multiple_of(head_of((x + k) % 4, yh, dest_core) * 256, 256)
                src = w.at[:, pl.ds(first, 256)]
            if j < 7:
                index = 7 * passed + j
                dev = (c, head_of((x + k) % 4, yh, dest_core))
                go(remote(src, w_cols.at[slot], w_ss.at[index], w_rs.at[index], dev))
            else:
                w_cols[slot] = src[...]

    def wait_w():
        for passed in range(2):
            for j, (k, other) in enumerate(w_steps):
                core = (1 - co) if other else co
                slot = head_of((x + 4 - k) % 4, 1 - yh if passed else yh, core)
                index = 7 * passed + j
                dev = (c, head_of((x + k) % 4, yh, core))
                here = w_cols.at[slot]
                remote(here, here, w_ss.at[index], w_rs.at[index], dev).wait_recv()

    def add_pieces(pieces, first=False):
        for i in range(2):
            rows = slice(i * BLOCK, (i + 1) * BLOCK)
            total = jnp.zeros((BLOCK, HEAD_DIM), F32) if first else do_acc[rows, :]
            for p in pieces:
                columns = pl.ds(pl.multiple_of(p * 256, 256), 256)
                total = total + nt(cot_all[p, rows], w[:, columns])
            do_acc[rows, :] = total

    empty = (
        jnp.full((1, BLOCK), EMPTY, F32),
        jnp.zeros((1, BLOCK), F32),
        jnp.zeros((HEAD_DIM, BLOCK), F32),
    )
    transpose_slot(z)
    for i in range(2):
        state = forward_tile(kns[i], vnt[i], qs[0, i], empty)
        if i == 1:
            state = forward_tile(kv[z, 0, 0], vt[z, 0], qs[0, 1], state)
        put_state(0, i, state)
        put_state(1, i, empty)
    def slot_tasks(slot):
        def first():
            transpose_slot(slot)
            forward_pair(0, slot)

        return [first, lambda: forward_pair(1, slot)]

    def late_queries():
        q_copy.wait_recv()
        forward_pair(1, z)

    cot_args = (cot_all, c_ss, c_rs)
    hooks = {
        (1, 2): lambda: gather_second(*cot_args, 0),
        (1, 3): lambda: [gather_pass(*cot_args, 0, d) for d in range(2)],
        (2, 1): lambda: [gather_second(*cot_args, 1), gather_near(*cot_args, 0)],
        (2, 2): lambda: gather_pass(*cot_args, 1, 0),
        (2, 0): lambda: send_w_across(),
        (3, 0): lambda: gather_far(*cot_args, 0),
        (3, 1): lambda: [
            gather_pass(*cot_args, 1, 1),
            add_pieces([h, near_slot(0, 0), near_slot(0, 1)], True),
        ],
        (3, 2): lambda: [
            gather_end(*cot_args, 0, 2),
            add_pieces([yh_head, sib_slots[0], sib_slots[1]]),
        ],
        (3, 3): lambda: gather_near(*cot_args, 1),
        (4, 0): lambda: [
            gather_end(*cot_args, 2, 4),
            add_pieces([x_head(2, yh, co), sib_slots[2], sib_slots[3]]),
        ],
        (4, 1): lambda: add_pieces([near_slot(1, 0), near_slot(1, 1)]),
    }
    tasks = []
    for s in range(1, 5):
        events = [(t, i) for t in range(2) for i in range(2)]
        if s == 4:
            events = [(t, i) for i in range(2) for t in range(2)]
        for n, (t, i) in enumerate(events):
            for d in range(2):
                if s < 4 or t == d:
                    kv_wait(d, s, t, i)
                    if s < 3 or (s == 3 and t == d):
                        go(kv_copy(d, s + 1, t, i))
            if (s, n) in hooks:
                hooks[s, n]()
            if tasks:
                tasks.pop(0)()
        if s == 1:
            tasks.append(late_queries)
        if s < 4:
            tasks += slot_tasks((z + NZ - s) % NZ) + slot_tasks((z + s) % NZ)
    while tasks:
        tasks.pop(0)()
    slot = (z + 4) % NZ
    transpose_slot(slot)
    forward_pair(1, slot)
    for i in range(2):
        acc_out[i] = acc[1, i].astype(BF)
    ml_copy = y_copy(1, ml.at[1], ml_in)
    acc_copies = [y_copy((2, 6)[i], acc_out.at[i], acc_in.at[i]) for i in range(2)]
    go(ml_copy)
    for copy in acc_copies:
        go(copy)
    gather_far(*cot_args, 1)
    gather_end(*cot_args, 4, 8)
    add_pieces([x_head(2, 1 - yh, co)] + sib_slots[4:])
    for i in range(2):
        dos[0, i] = do_acc[i * BLOCK : (i + 1) * BLOCK, :].astype(BF)
    do_copy = y_copy(3, dos.at[0], dos.at[1])
    go(do_copy)
    forward_pair(0, (z + 4) % NZ)

    for i in range(2):
        dos_t[i] = dos[0, i].T.astype(F32)
    ml_copy.wait_recv()
    shares = []
    for i in range(2):
        own_max, own_sum, other_max, other_sum = ml[0, i], ml[0, 2 + i], ml_in[i], ml_in[2 + i]
        top = jnp.maximum(own_max, other_max)
        own_part = jnp.exp2((own_max - top) * SCALE2)
        other_part = jnp.exp2((other_max - top) * SCALE2)
        total = own_sum * own_part + other_sum * other_part
        ld[0, i] = top * SCALE2 + jnp.log2(total)
        shares.append(((own_part / total)[:1], (other_part / total)[:1]))
    for i, (own_part, other_part) in enumerate(shares):
        acc_copies[i].wait_recv()
        attended_t = (acc[0, i] * own_part + acc_in[i].astype(F32) * other_part).astype(BF)
        att_t[:, i * BLOCK : (i + 1) * BLOCK] = attended_t
        row_dot = jnp.sum(dos_t[i] * attended_t.astype(F32), axis=0, keepdims=True)
        ld[0, 2 + i] = jnp.broadcast_to(row_dot, (8, BLOCK))
    ld_copy = y_copy(4, ld.at[0], ld.at[1])
    go(ld_copy)
    send_w(0)
    for i in range(2):
        rows = slice(i * BLOCK, (i + 1) * BLOCK)
        att_all[h, rows, :] = att_t[:, rows].T
    gather_begin(att_all, a_ss, a_rs)

    def gy_slot(j):
        return (z + (4, 3, 5, 2, 6, 1, 7, 0)[j]) % NZ

    gy_copies = []

    def send_gy(first, last):
        for j in range(first, last):
            slot = gy_slot(j)
            gy_out[j] = nn(att_t[...], cot_all[(1 - yl) * NZ + slot]).astype(BF)
            gy_copies.append(remote(gy_out.at[j], gy_in.at[j], gy_ss.at[j], gy_rs.at[j], y_dev))
            go(gy_copies[-1])

    send_gy(0, 3)

    for i in range(2):
        key_term, value_term, query_term = backward_tile(
            kns[i], vns[i], knt[i], qs[0, i], dos[0, i], ld[0, i][:1], ld[0, 2 + i][:1]
        )
        stage[0, i] = (key_term * SCALE).astype(BF)
        stage[1, i] = value_term.astype(BF)
        dq[0, i] = query_term
        dq[1, i] = jnp.zeros_like(query_term)

    def unsort(index, out):
        for b in range(2):
            rows = jnp.where(swap, stage[index, 1 - b], stage[index, b])
            finals[index, b * BLOCK : (b + 1) * BLOCK, :] = rows
        put(finals.at[index], out)

    unsort(0, gkn)
    unsort(1, gvn)

    def backward_pair(par, d, qd, slot, same=False):
        low, high = (
            backward_tile(
                kv[slot, 0, 0], kv[slot, 1, 0], kt[slot, 0],
                qs[qd, 1], dos[qd, 1], ld[qd, 1][:1], ld[qd, 3][:1],
            ),
            None,
        )
        if same:
            cb[par, d, 0, 0] = low[0]
            cb[par, d, 1, 0] = low[1]
            cb[par, d, 0, 1] = jnp.zeros_like(low[0])
            cb[par, d, 1, 1] = jnp.zeros_like(low[1])
            dq[qd, 1] += low[2]
            return
        pick = seen_high(qd, slot)

        def chosen(first, second):
            return jnp.where(pick, second, first)

        high = backward_tile(
            chosen(kv[slot, 0, 0], kv[slot, 0, 1]),
            chosen(kv[slot, 1, 0], kv[slot, 1, 1]),
            chosen(kt[slot, 0], kt[slot, 1]),
            chosen(qs[qd, 0], qs[qd, 1]),
            chosen(dos[qd, 0], dos[qd, 1]),
            chosen(ld[qd, 0][:1], ld[qd, 1][:1]),
            chosen(ld[qd, 2][:1], ld[qd, 3][:1]),
        )
        to_high = pick.astype(F32)
        to_low = 1.0 - to_high
        for t in range(2):
            new_low = low[t] + high[t] * to_low
            new_high = high[t] * to_high
            if qd == 0:
                cb[par, d, t, 0] = new_low
                cb[par, d, t, 1] = new_high
            else:
                cb[par, d, t, 0] += new_low
                cb[par, d, t, 1] += new_high
        dq[qd, 0] += high[2] * to_low
        dq[qd, 1] += low[2] + high[2] * to_high

    def contribution_tasks(s):
        par = s % 2
        if s in (0, 4):
            slot = (z + 4 - s) % NZ
            pairs = [(0, 0, slot, s == 4), (0, 1, slot)]
        else:
            slots = [(z + 4 - s) % NZ, (z + NZ - 4 + s) % NZ]
            pairs = [(d, qd, slots[d]) for d in range(2) for qd in range(2)]
        return [functools.partial(backward_pair, par, *pair) for pair in pairs]

    factors = (SCALE, 1.0)

    def rs_copy(d, s, t, i):
        at = (d, s, t, i)
        return remote(rs_out.at[at], rs_in.at[at], r_ss.at[at], r_rs.at[at], z_dev[d])

    def g_copy(d, s):
        rows = pl.ds(64 * d, 64) if s == 0 else pl.ds(0, 128)
        return remote(
            g_out.at[d, s, rows], g_in.at[d, s, rows], g_ss.at[d, s], g_rs.at[d, s], z_dev[d]
        )

    def g_piece(j):
        gy_copies[j].wait_recv()
        own = nn(att_t[...], cot_all[yl * NZ + gy_slot(j)])
        return own + gy_in[j].astype(F32)

    own, other = contribution_tasks(0)
    own()
    do_copy.wait_recv()
    ld_copy.wait_recv()
    other()
    for t in range(2):
        for i in range(2):
            rs_out[t, 0, t, i] = (cb[0, 0, t, i] * factors[t]).astype(BF)
            go(rs_copy(t, 0, t, i))
    send_gy(3, 8)
    send_w(1)

    def rs_step(s, tasks):
        for t, i, d in [(t, i, d) for t in range(2) for i in range(2) for d in range(2)]:
            term = cb[s % 2, d, t, i] * factors[t]
            if s > 1 or t == d:
                rs_copy(d, s - 1, t, i).wait_recv()
                term = term + rs_in[d, s - 1, t, i].astype(F32)
            rs_out[d, s, t, i] = term.astype(BF)
            go(rs_copy(d, s, t, i))
            if d and tasks:
                tasks.pop(0)()

    def g_step(s):
        if s == 0:
            piece = g_piece(0).astype(BF)
            for d in range(2):
                g_out[d, 0] = piece
                go(g_copy(d, 0))
            return
        for d in range(2):
            piece = g_piece(2 * s - 1 + d)
            g_copy(d, s - 1).wait_recv()
            if s == 1:
                half = slice(64 * d, 64 * d + 64)
                rest = slice(64 - 64 * d, 128 - 64 * d)
                g_out[d, 1, half] = (piece[half] + g_in[d, 0, half].astype(F32)).astype(BF)
                g_out[d, 1, rest] = piece[rest].astype(BF)
            else:
                g_out[d, s] = (piece + g_in[d, s - 1].astype(F32)).astype(BF)
            go(g_copy(d, s))

    for task in contribution_tasks(1):
        task()
    g_step(0)
    rs_step(1, contribution_tasks(2))
    g_step(1)
    gather_second(att_all, a_ss, a_rs, 0)
    gather_second(att_all, a_ss, a_rs, 1)
    gather_pass(att_all, a_ss, a_rs, 0, 0)
    gather_pass(att_all, a_ss, a_rs, 0, 1)
    gather_near(att_all, a_ss, a_rs, 0)
    rs_step(2, contribution_tasks(3))
    g_step(2)
    gather_pass(att_all, a_ss, a_rs, 1, 0)
    gather_pass(att_all, a_ss, a_rs, 1, 1)
    gather_near(att_all, a_ss, a_rs, 1)
    gather_far(att_all, a_ss, a_rs, 0)
    older = len(sends)
    rs_step(3, contribution_tasks(4))
    g_step(3)
    gather_far(att_all, a_ss, a_rs, 1)
    for copy in sends[:older]:
        copy.wait_send()
    del sends[:older]

    for i in range(2):
        dq_out[i] = (dq[1, i] * SCALE).astype(BF)
    dq_copy = y_copy(5, dq_out, dq_in)
    go(dq_copy)

    gather_end(att_all, a_ss, a_rs)
    wait_w()
    total = nn(att_all[0], w_cols[0])
    for p in range(1, 16):
        total = total + nn(att_all[p], w_cols[p])
    cotm[...] = total.astype(BF)
    for b in range(2):
        mixed_final[b * BLOCK : (b + 1) * BLOCK, :] = in_order(cotm, b)
    put(mixed_final, mixed)

    dq_copy.wait_recv()
    for i in range(2):
        stage[2, i] = (dq[0, i] * SCALE + dq_in[i].astype(F32)).T.astype(BF)
    unsort(2, gq)

    for t in range(2):
        for i in range(2):
            for d in range(2):
                rs_copy(d, 3, t, i).wait_recv()
            stage[3 + t, i] = (
                cb[0, 0, t, i] * factors[t]
                + rs_in[0, 3, t, i].astype(F32)
                + rs_in[1, 3, t, i].astype(F32)
            ).astype(BF)
        unsort(3 + t, (gkc, gvc)[t])

    piece = g_piece(7)
    for d in range(2):
        g_copy(d, 3).wait_recv()
        piece = piece + g_in[d, 3].astype(F32)
    gw_final[...] = piece
    put(gw_final, gw)

    for copy in sends:
        copy.wait_send()
    for store in stores:
        store.wait()


def hand_on(*refs):
    for i in range(7):
        refs[7 + i][...] = refs[i][...]


def per_device(q, kn, vn, kc, vc, w, cot, noise_mask, block_order):
    vmem = pl.BlockSpec(memory_space=pltpu.VMEM)
    smem = pl.BlockSpec(memory_space=pltpu.SMEM)
    rows, width = q.shape
    blk = (BLOCK, HEAD_DIM)
    tblk = (HEAD_DIM, BLOCK)
    dma = pltpu.SemaphoreType.DMA
    narrow = jax.ShapeDtypeStruct((rows, width), BF)
    scratch = [
        *[pltpu.VMEM((rows, width), BF)] * 5,
        pltpu.VMEM(w.shape, BF),
        pltpu.VMEM(cot.shape, BF),
        pltpu.VMEM((2, 2) + blk, BF),
        pltpu.VMEM((2,) + blk, BF),
        pltpu.VMEM((2,) + blk, BF),
        pltpu.VMEM((NZ, 2, 2) + blk, BF),
        pltpu.VMEM((NZ, 2) + tblk, BF),
        pltpu.VMEM((NZ, 2) + tblk, BF),
        pltpu.VMEM((2,) + tblk, BF),
        pltpu.VMEM((2,) + tblk, BF),
        pltpu.VMEM((2, 4, 8, BLOCK), F32),
        pltpu.VMEM((4, 8, BLOCK), F32),
        pltpu.VMEM((2, 2) + tblk, F32),
        pltpu.VMEM((2,) + tblk, BF),
        pltpu.VMEM((2,) + tblk, BF),
        pltpu.VMEM((rows, 256), BF),
        pltpu.VMEM((16, rows, 256), BF),
        pltpu.VMEM((16, HEAD_DIM, 256), BF),
        pltpu.VMEM((4, HEAD_DIM, 512), BF),
        pltpu.VMEM((HEAD_DIM, rows), BF),
        pltpu.VMEM((16, rows, HEAD_DIM), BF),
        pltpu.VMEM((rows, HEAD_DIM), F32),
        pltpu.VMEM((2, 2) + blk, BF),
        pltpu.VMEM((2,) + tblk, F32),
        pltpu.VMEM((2, 4, 8, BLOCK), F32),
        pltpu.VMEM((2, 2) + tblk, F32),
        pltpu.VMEM((2,) + tblk, BF),
        pltpu.VMEM((2,) + tblk, BF),
        pltpu.VMEM((2, 2, 2, 2) + blk, F32),
        pltpu.VMEM((2, 4, 2, 2) + blk, BF),
        pltpu.VMEM((2, 4, 2, 2) + blk, BF),
        pltpu.VMEM((8, HEAD_DIM, 256), BF),
        pltpu.VMEM((8, HEAD_DIM, 256), BF),
        pltpu.VMEM((2, 4, HEAD_DIM, 256), BF),
        pltpu.VMEM((2, 4, HEAD_DIM, 256), BF),
        pltpu.VMEM((5, 2) + blk, BF),
        pltpu.VMEM((5, rows, width), BF),
        pltpu.VMEM(cot.shape, BF),
        pltpu.VMEM((HEAD_DIM, 256), F32),
        dma((7,)), dma((7,)),
        dma((2, 4, 2, 2)), dma((2, 4, 2, 2)),
        dma((7,)), dma((7,)),
        dma((8,)), dma((8,)),
        dma((22,)), dma((22,)),
        dma((22,)), dma((22,)),
        dma((4,)), dma((4,)),
        dma((14,)), dma((14,)),
        dma((2, 4, 2, 2)), dma((2, 4, 2, 2)),
        dma((2, 4)), dma((2, 4)),
    ]
    shapes = (
        jax.ShapeDtypeStruct(cot.shape, BF),
        narrow, narrow, narrow, narrow, narrow,
        jax.ShapeDtypeStruct((HEAD_DIM, 256), F32),
    )

    outs = pl.pallas_call(
        kernel,
        out_shape=tuple(pltpu.VMEM(shape.shape, shape.dtype) for shape in shapes),
        in_specs=[smem, vmem] + [pl.BlockSpec(memory_space=pltpu.HBM)] * 7,
        scratch_shapes=scratch,
        compiler_params=pltpu.CompilerParams(
            collective_id=0, has_side_effects=True, vmem_limit_bytes=56 * 2**20
        ),
        name="block_attention",
    )(block_order, noise_mask.reshape(4, 128), q, kn, vn, kc, vc, w, cot)
    return pl.pallas_call(
        hand_on,
        out_shape=shapes,
        in_specs=[vmem] * 7,
        out_specs=(vmem,) * 7,
        compiler_params=pltpu.CompilerParams(vmem_limit_bytes=8 * 2**20),
        name="hand_on",
    )(*outs)


def solution(mesh):
    spread = P("ctx", "head")
    return jax.shard_map(
        per_device,
        mesh=mesh,
        in_specs=(spread,) * 5 + (P("head", None), spread, P("ctx"), P()),
        out_specs=(spread,) * 6 + (P("head", "ctx"),),
        check_vma=False,
    )
```
